128 devices in a mesh: blk: 16 (over z, x_hi, core), dp: 8 (over y, x_lo).
Axes of the slice: x: 4 (x_hi: 2, x_lo: 2; x = x_hi * 2 + x_lo), y: 4, z: 4, core: 2. Of those that a mesh axis runs over, the one named last changes fastest.
Arguments:
- tokens: bfloat16 [65536, 2048], P(('blk', 'dp')), may hold values from -24 to 24
- segment_ids: int32 [128, 512], P(('blk', 'dp')), may hold values from -1 to 31, as said below
- owners: int32 [128, 32], P(('blk', 'dp')), may hold values from -1 to 127, as said below
- images: bfloat16 [2048, 1152], P(('blk', 'dp')), may hold values from -6 to 6
- weight: bfloat16 [2048, 2048], replicated, may hold values from -0.125 to 0.125
- gain: float32 [2048], replicated, may hold values from 0.25 to 1.75
- head: bfloat16 [2048, 1152], replicated, may hold values from -0.125 to 0.125
- logit_params: float32 [2], replicated, as said below
Outputs:
- loss: float32 [2048], P(('blk', 'dp'))
- d_tokens: bfloat16 [65536, 2048], P(('blk', 'dp'))
- d_weight: float32 [2048, 2048], P(('blk', 'dp'))
- d_gain: float32 [2048], replicated
- d_images: float32 [2048, 1152], P(('blk', 'dp'))
The draws below stay inside these ranges and needn't reach their ends.
Inputs may be any that keep to these rules, and one draw needn't show every extreme that they name: `owners`: entry c of device row r is -1 for an empty caption slot, else the slot, among the 128 images of the devices with the same blk index, of the image that caption describes; over those devices every slot is named exactly once. The captions of one device name at most 4 slots of any one device (slot // 16), and in every group some device names exactly 4 of every device's slots. `segment_ids`: A caption slot holds tokens exactly when its owners entry is not -1; those tokens are one run of 1 to 32 positions, the runs in slot order from position 0, and -1 after the last run. `logit_params`: entry 0 is the log temperature, entry 1 the bias.
All inputs are finite; a program needn't handle non-finite values.
Results may differ from the reference program's by a relative error of at most 0.019.
Values may be sent and summed in bfloat16 or wider, within the bound.
A program may use at most 128 MiB of HBM per device.

```python
import jax
import jax.numpy as jnp
from jax import lax

DT = 2048
E = 1152
B_DEV = 16
LMAX = 32
ROWS = 512
CAPS = 32
GROUP = 128
TOTAL = 2048
N_BLK = 16
N_DP = 8


def packing_draw(key):
    capp = 2 * B_DEV // N_DP

    def one_group(gkey):
        key_roles, key_slots, key_order, key_lens = jax.random.split(gkey, 4)
        roles = jax.random.permutation(key_roles, N_DP).astype(jnp.int32)
        per_peer = jnp.where(roles == 0, 2 * B_DEV // N_DP, jnp.where(roles <= 2, B_DEV // (2 * N_DP), B_DEV // N_DP)).astype(jnp.int32)
        offsets = jnp.cumsum(per_peer) - per_peer
        slot_perm = jax.vmap(lambda k: jax.random.permutation(k, B_DEV))(jax.random.split(key_slots, N_DP)).astype(jnp.int32)
        within = jnp.arange(capp, dtype=jnp.int32)
        picks = jnp.minimum(offsets[:, None, None] + within[None, None, :], B_DEV - 1)
        picks = jnp.broadcast_to(picks, (N_DP, N_DP, capp))
        dest = jnp.broadcast_to(jnp.arange(N_DP, dtype=jnp.int32)[None, :, None], (N_DP, N_DP, capp))
        chosen = slot_perm[dest, picks]
        live = within[None, None, :] < per_peer[:, None, None]
        raw = jnp.where(live, dest * B_DEV + chosen, -1).reshape(N_DP, N_DP * capp)
        order = jax.vmap(lambda k: jax.random.permutation(k, N_DP * capp))(jax.random.split(key_order, N_DP))
        owned = jnp.take_along_axis(raw, order.astype(jnp.int32), axis=1)
        cap_len = jnp.where(roles == 0, LMAX // 2, LMAX).astype(jnp.int32)
        lens = jax.random.randint(key_lens, (N_DP, CAPS), 1, cap_len[:, None] + 1).astype(jnp.int32)
        lens = jnp.where(owned >= 0, lens, 0)
        starts = jnp.cumsum(lens, axis=1) - lens
        position = jnp.arange(ROWS, dtype=jnp.int32)
        inside = (position[None, None, :] >= starts[:, :, None]) & (position[None, None, :] < (starts + lens)[:, :, None])
        seg = jnp.sum(inside.astype(jnp.int32) * (jnp.arange(CAPS, dtype=jnp.int32)[None, :, None] + 1), axis=1) - 1
        return (owned, seg)
    owned, seg = jax.vmap(one_group)(jax.random.split(key, N_BLK))
    return (owned.reshape(N_BLK * N_DP, CAPS).astype(jnp.int32), seg.reshape(N_BLK * N_DP, ROWS).astype(jnp.int32))


def draw_owners(key, part):
    owned, seg = packing_draw(key)
    return owned


def draw_segment_ids(key, part):
    owned, seg = packing_draw(key)
    return seg


def draw_logit_params(key, part):
    key = jax.random.fold_in(key, 7)
    values = jax.random.uniform(key, (2,), jnp.float32)
    return jnp.stack([1.0 + 0.8 * values[0], -3.0 + 2.0 * values[1]]).astype(jnp.float32)


def spiked(drawn, key, source, target, shards_of, factor):
    owner, partner = [(jnp.arange(drawn.shape[axis_at]) // (drawn.shape[axis_at] // shards_of)).reshape([-1 if axis == axis_at else 1 for axis in range(drawn.ndim)]) for axis_at in (source, target)]
    chosen = jax.random.permutation(key, shards_of)[partner]
    strong = (owner == chosen) | (owner == (partner + shards_of // 2) % shards_of)
    return jnp.where(strong, factor * drawn, drawn)


def steps_of(own_key, dims, shards, low, top_value):
    level = 1.0
    for dim, blocks in shards:
        heights = jax.random.uniform(jax.random.fold_in(jax.random.fold_in(own_key, 6), dim), (blocks,), jnp.float32, low / len(shards), top_value / len(shards))
        level = level * jnp.repeat(jnp.exp(heights), dims[dim] // blocks).reshape((-1,) + (1,) * (len(dims) - 1 - dim))
    return level


def scatter_about(stream_key, extent, deviation, bound, pieces=(), kind=jnp.bfloat16):
    level = steps_of(stream_key, extent, pieces, -0.22, 0.18) if pieces else 1.0
    drawn = jax.random.normal(stream_key, extent, jnp.float32) * deviation * level
    return jnp.minimum(jnp.maximum(drawn, -bound), bound).astype(kind)


def noise_with(rng, extent, scale, reach, cuts, heavy, kind=jnp.bfloat16):
    entries = scale * jax.random.normal(rng, extent, jnp.float32)
    if cuts:
        entries = entries * steps_of(rng, extent, cuts, -0.22, 0.18)
    return jnp.clip(spiked(entries, jax.random.fold_in(rng, 3), *heavy), -reach, reach).astype(kind)


def setup_inputs(seed: int = 0) -> dict:
    key_list = jax.random.split(jax.random.key(seed), 9)
    return {
        "tokens": noise_with(key_list[0], (N_BLK * N_DP * ROWS, DT), 1.0, 24.0, ((0, 128),), (0, 1, 128, 5.5)),
        "segment_ids": draw_segment_ids(jax.random.fold_in(key_list[8], 71), 0),
        "owners": draw_owners(jax.random.fold_in(key_list[8], 71), 0),
        "images": scatter_about(key_list[3], (TOTAL, E), 1.0, 6.0, ((0, 128),)),
        "weight": scatter_about(key_list[4], (DT, DT), DT ** -0.5, 0.125),
        "gain": jnp.clip(1.0 + 0.15 * jax.random.normal(key_list[5], (DT,), jnp.float32), 0.25, 1.75),
        "head": scatter_about(key_list[6], (DT, E), DT ** -0.5, 0.125),
        "logit_params": draw_logit_params(jax.random.fold_in(key_list[8], 71), 0),
    }


def reference(tokens, segment_ids, owners, images, weight, gain, head, logit_params):
    f32 = jnp.float32
    bf16 = jnp.bfloat16
    devs = N_BLK * N_DP
    x = tokens.astype(f32)
    inv_rms = lax.rsqrt(lax.optimization_barrier(jnp.mean(x * x, axis=1, keepdims=True)) + 1e-06)
    normed = (x * inv_rms * gain).astype(bf16)
    hidden = (x + jnp.dot(normed, weight, preferred_element_type=f32)).astype(bf16)
    hidden_dev = hidden.reshape(devs, ROWS, DT)
    slots = jnp.arange(CAPS, dtype=jnp.int32)
    counts_all = jnp.maximum(lax.optimization_barrier(jnp.sum((segment_ids[:, None, :] == slots[None, :, None]).astype(f32), axis=2)), 1.0)

    def pool_one(pair):
        seg, hid, cnt = pair
        select = (seg[None, :] == slots[:, None]).astype(bf16)
        return (jnp.dot(select, hid, preferred_element_type=f32) / cnt[:, None]).astype(bf16)
    pooled = lax.map(pool_one, (segment_ids, hidden_dev, counts_all))
    group = (jnp.arange(devs, dtype=jnp.int32) // N_DP)[:, None]
    text_index = jnp.where(owners >= 0, group * GROUP + owners, TOTAL).astype(jnp.int32)
    texts_pooled = jnp.zeros((TOTAL, DT), bf16).at[text_index.reshape(-1)].set(pooled.reshape(-1, DT), mode='drop')
    proj = jnp.dot(texts_pooled, head, preferred_element_type=f32)
    scale_inv = lax.rsqrt(lax.optimization_barrier(jnp.sum(proj * proj, axis=1, keepdims=True)) + 1e-06)
    text_unit = proj * scale_inv
    text_embed = text_unit.astype(bf16)
    img = images.astype(f32)
    img_inv = lax.rsqrt(lax.optimization_barrier(jnp.sum(img * img, axis=1, keepdims=True)) + 1e-06)
    img_unit = img * img_inv
    img_embed = img_unit.astype(bf16)
    scale = jnp.exp(logit_params[0])
    bias = logit_params[1]
    logits = scale * jnp.dot(img_embed, text_embed.T, preferred_element_type=f32) + bias
    ids = jnp.arange(TOTAL, dtype=jnp.int32)
    sign = jnp.where(ids[:, None] == ids[None, :], 1.0, -1.0).astype(f32)
    loss = lax.optimization_barrier(jnp.sum(jax.nn.softplus(-sign * logits), axis=1)) / TOTAL
    coef = (-scale * sign * jax.nn.sigmoid(-sign * logits)).astype(bf16)
    dimg = jnp.dot(coef, text_embed, preferred_element_type=f32)
    dtext = jnp.dot(coef.T, img_embed, preferred_element_type=f32)
    d_images = img_inv * (dimg - img_unit * lax.optimization_barrier(jnp.sum(img_unit * dimg, axis=1, keepdims=True)))
    dproj = (scale_inv * (dtext - text_unit * lax.optimization_barrier(jnp.sum(text_unit * dtext, axis=1, keepdims=True)))).astype(bf16)
    dpooled_text = jnp.dot(dproj, head.T, preferred_element_type=f32).astype(bf16)
    safe = jnp.minimum(text_index, TOTAL - 1)
    dpooled = jnp.where((owners >= 0)[:, :, None], dpooled_text[safe].astype(f32), 0.0)
    dcap = (dpooled / counts_all[:, :, None]).astype(bf16)

    def spread_one(pair):
        seg, piece = pair
        select = (seg[None, :] == slots[:, None]).astype(bf16)
        return jnp.dot(select.T, piece, preferred_element_type=f32).astype(bf16)
    dhidden = lax.map(spread_one, (segment_ids, dcap)).reshape(devs * ROWS, DT)
    dnorm = jnp.dot(dhidden, weight.T, preferred_element_type=f32)
    d_weight = jnp.dot(normed.T, dhidden, preferred_element_type=f32)
    scaled = gain * dnorm
    dx = inv_rms * scaled - x * inv_rms * inv_rms * inv_rms * lax.optimization_barrier(jnp.mean(x * scaled, axis=1, keepdims=True))
    d_tokens = (dhidden.astype(f32) + dx).astype(bf16)
    d_gain = lax.optimization_barrier(jnp.sum(x * inv_rms * dnorm, axis=0))
    return (loss, d_tokens, d_weight, d_gain, d_images)
```

```python
import functools

import jax
import jax.numpy as jnp
from jax import lax
from jax.experimental import pallas as pl
from jax.experimental.pallas import tpu as pltpu
from jax.sharding import PartitionSpec as P

f32 = jnp.float32
bf16 = jnp.bfloat16
MESH = pl.DeviceIdType.MESH

DT = 2048
E = 1152
ROWS = 512
CAPS = 32
NB = 16
ND = 8
TOTAL = 2048
PW = E + 128
PARTS = 3
PC = E // PARTS
ORDERS = (("x", "y", "z"), ("y", "z", "x"), ("z", "x", "y"))
TN = 512


def mm(a, b):
    return lax.dot_general(a, b, (((1,), (0,)), ((), ())), preferred_element_type=f32)


def mm_nt(a, b):
    return lax.dot_general(a, b, (((1,), (1,)), ((), ())), preferred_element_type=f32)


def split2(v):
    hi = v.astype(bf16)
    return hi, (v - hi.astype(f32)).astype(bf16)


def iota(shape, dim):
    return lax.broadcasted_iota(jnp.int32, shape, dim)


def kernel(
    tok_hbm, w_hbm, head_hbm, seg_ref, own_ref, img_ref, gain_ref, lp_ref,
    loss_out, dtok_hbm, dw_out, dgain_out, dimg_out,
    tok, wv, headv, img, lcol, segt, invc, xs, xp, npst, pooled, asrc, arcv, tbuf, dcap, stack,
    stage, bacc, rsacc, c3s, c3r, lbuf, gsrc, gbuf, g2,
    ld_sem, w_sem, st_sem,
    i_send, i_recv, ic_send, ic_recv, t_send, t_recv, tc_send, tc_recv, a_send, a_recv,
    c_send, c_recv, l_send, l_recv, g_send, g_recv, h_send, h_recv,
):
    b = lax.axis_index("blk")
    d = lax.axis_index("dp")
    z, xh, core = b // 4, (b // 2) % 2, b % 2
    y, xl = d // 2, d % 2
    x = xh * 2 + xl
    sib = (b + 1 - 2 * core, d)

    loads = []
    for i in range(4):
        cp = pltpu.make_async_copy(
            tok_hbm.at[pl.ds(i * 128, 128), :], tok.at[pl.ds(i * 128, 128), :], ld_sem.at[i]
        )
        cp.start()
        loads.append(cp)
    wloads = []
    for i in range(DT // TN):
        cp = pltpu.make_async_copy(
            w_hbm.at[:, pl.ds(i * TN, TN)], wv.at[:, pl.ds(i * TN, TN)], w_sem.at[i]
        )
        cp.start()
        wloads.append(cp)
    hload = pltpu.make_async_copy(head_hbm, headv, ld_sem.at[4])
    hload.start()

    barrier = pltpu.get_barrier_semaphore()
    for k in range(1, ND):
        pl.semaphore_signal(barrier, inc=1, device_id=(b, (d + k) % ND), device_id_type=MESH)
    for k in range(1, NB):
        pl.semaphore_signal(barrier, inc=1, device_id=((b + k) % NB, d), device_id_type=MESH)
    pl.semaphore_signal(
        barrier, inc=1, device_id=(z * 4 + (1 - xh) * 2 + core, y * 2 + 1 - xl), device_id_type=MESH
    )

    im = img_ref[...].astype(f32)
    img_inv = lax.rsqrt(jnp.sum(im * im, axis=1, keepdims=True) + 1e-06)
    img_unit = im * img_inv
    img[z, xh, core, y, xl] = img_unit.astype(bf16)

    pl.semaphore_wait(barrier, NB + ND - 1)

    sends = []

    def region(p, at):
        def pick(name):
            return slice(None) if at[name] is None else at[name]

        xx = at["x"]
        return img.at[
            pick("z"),
            slice(None) if xx is None else xx // 2,
            at["core"],
            pick("y"),
            slice(None) if xx is None else xx % 2,
            :,
            pl.ds(p * PC, PC),
        ]

    here = {"x": x, "y": y, "z": z, "core": core}

    def device(at):
        return (at["z"] * 4 + (at["x"] // 2) * 2 + at["core"], at["y"] * 2 + at["x"] % 2)

    def ring_copy(p, s, k, done, where, to):
        at = dict(where)
        for name in done:
            at[name] = None
        ref = region(p, at)
        return pltpu.make_async_remote_copy(
            src_ref=ref, dst_ref=ref, send_sem=i_send.at[p, s, k], recv_sem=i_recv.at[p, s, k],
            device_id=device(to), device_id_type=MESH,
        )

    def ring_send(p, s):
        order = ORDERS[p]
        axis, done = order[s], order[:s]
        for k in range(3):
            to = dict(here)
            to[axis] = (here[axis] + k + 1) % 4
            cp = ring_copy(p, s, k, done, here, to)
            cp.start()
            sends.append(cp)

    def ring_wait(p, s, k):
        order = ORDERS[p]
        axis, done = order[s], order[:s]
        frm = dict(here)
        frm[axis] = (here[axis] + 3 - k) % 4
        ring_copy(p, s, k, done, frm, frm).wait_recv()

    def core_copy(p, q, own):
        order = ORDERS[p]
        at = dict(here)
        for name in order[:2]:
            at[name] = None
        if q:
            at[order[2]] = (here[order[2]] + 4 - q) % 4
        if not own:
            at["core"] = 1 - core
        ref = region(p, at)
        return pltpu.make_async_remote_copy(
            src_ref=ref, dst_ref=ref, send_sem=ic_send.at[p, q], recv_sem=ic_recv.at[p, q],
            device_id=sib, device_id_type=MESH,
        )

    def core_send(p, q):
        cp = core_copy(p, q, True)
        cp.start()
        sends.append(cp)

    for p in range(PARTS):
        ring_send(p, 0)

    segf = seg_ref[...].astype(f32)
    segt[...] = jnp.broadcast_to(segf, (128, ROWS)).T
    lane = iota((128, 128), 1)
    cap_of = (lane % CAPS).astype(f32)
    kind = lane // CAPS

    def token_rows(i):
        loads[i].wait()
        rows = pl.ds(i * 128, 128)
        xx = tok[rows, :].astype(f32)
        inv = lax.rsqrt(jnp.sum(xx * xx, axis=1, keepdims=True) * (1.0 / DT) + 1e-06)
        invc[rows, :] = inv
        hi = inv.astype(bf16).astype(f32)
        lo = inv - hi
        val = jnp.where(kind == 0, 1.0, jnp.where(kind == 2, lo, hi))
        lcol[rows, :] = jnp.where(segt[rows, :] == cap_of, val, 0.0)

    token_rows(0)
    token_rows(1)
    for p in range(PARTS):
        for k in range(3):
            ring_wait(p, 0, k)
        ring_send(p, 1)
    token_rows(2)
    token_rows(3)

    lrow = lcol[...].T.astype(bf16)
    gain = gain_ref[...]

    def pool_tile(i, _):
        cols = pl.ds(pl.multiple_of(i * TN, TN), TN)
        acc = mm(lrow, tok[:, cols])
        xs[:, cols] = acc[0:CAPS]
        xpt = acc[CAPS : 2 * CAPS] + acc[2 * CAPS : 3 * CAPS]
        xp[:, cols] = xpt
        hi, lo = split2(xpt * gain_ref[:, cols])
        npst[0:CAPS, cols] = hi
        npst[CAPS : 2 * CAPS, cols] = lo
        return 0

    lax.fori_loop(0, DT // TN, pool_tile, 0)

    for p in range(PARTS):
        for k in range(3):
            ring_wait(p, 1, k)
        ring_send(p, 2)
        core_send(p, 0)

    sel = (jnp.broadcast_to(segf, (CAPS, ROWS)) == iota((CAPS, ROWS), 0).astype(f32)).astype(f32)
    rcount = 1.0 / jnp.maximum(jnp.sum(sel, axis=1, keepdims=True), 1.0)
    ownf = own_ref[...].astype(f32)
    own_col = jnp.sum(
        jnp.where(iota((CAPS, CAPS), 0) == iota((CAPS, CAPS), 1), jnp.broadcast_to(ownf, (CAPS, CAPS)), 0.0),
        axis=1,
        keepdims=True,
    )

    for i in range(DT // TN):
        wloads[i].wait()
        cols = pl.ds(i * TN, TN)
        yy = mm(npst[...], wv[:, cols])
        pooled[:, cols] = ((xs[:, cols] + yy[0:CAPS] + yy[CAPS : 2 * CAPS]) * rcount).astype(bf16)

    hload.wait()
    proj = mm(pooled[...], headv[...])
    scale_inv = lax.rsqrt(jnp.sum(proj * proj, axis=1, keepdims=True) + 1e-06)
    text_unit = proj * scale_inv
    text = text_unit.astype(bf16)
    tbuf[b, :, 0:E] = text
    tbuf[b, :, E:PW] = jnp.broadcast_to(own_col, (CAPS, 128)).astype(bf16)
    factor = scale_inv * rcount
    for j in range(NB):
        cols = pl.ds(j * 128, 128)
        asrc[j] = (xp[:, cols] * gain_ref[:, cols] * factor).astype(bf16)
    arcv[b] = asrc[b]

    def text_peer(k, sign):
        dz, dx = (k + 1) // 2, (k + 1) % 2
        return ((z + 4 + sign * dz) % 4) * 4 + ((xh + dx) % 2) * 2 + core

    def text_copy(k, idx, to):
        return pltpu.make_async_remote_copy(
            src_ref=tbuf.at[idx], dst_ref=tbuf.at[idx], send_sem=t_send.at[k], recv_sem=t_recv.at[k],
            device_id=(to, d), device_id_type=MESH,
        )

    def text_core(k, idx):
        return pltpu.make_async_remote_copy(
            src_ref=tbuf.at[idx], dst_ref=tbuf.at[idx], send_sem=tc_send.at[k], recv_sem=tc_recv.at[k],
            device_id=sib, device_id_type=MESH,
        )

    for k in range(7):
        cp = text_copy(k, b, text_peer(k, 1))
        cp.start()
        sends.append(cp)
    cp = text_core(7, b)
    cp.start()
    sends.append(cp)
    for k in range(NB - 1):
        to = (b + k + 1) % NB
        cp = pltpu.make_async_remote_copy(
            src_ref=asrc.at[to], dst_ref=arcv.at[b], send_sem=a_send.at[k], recv_sem=a_recv.at[k],
            device_id=(to, d), device_id_type=MESH,
        )
        cp.start()
        sends.append(cp)

    for p in range(PARTS):
        for k in range(3):
            ring_wait(p, 2, k)
            core_send(p, k + 1)
    for k in range(7):
        frm = text_peer(k, -1)
        text_copy(k, frm, frm).wait_recv()
        cp = text_core(k, frm)
        cp.start()
        sends.append(cp)
    for p in range(PARTS):
        for q in range(4):
            core_copy(p, q, False).wait_recv()

    scale = jnp.exp(jnp.full((1, 128), lp_ref[0], f32))[:, 0:1]
    bias = jnp.full((1, 128), lp_ref[1], f32)[:, 0:1]

    def pair(dots, gid, first):
        ids = (iota((1, dots.shape[1]), 1) + first).astype(f32)
        sgn = jnp.where(gid == ids, 1.0, -1.0)
        arg = -sgn * (scale * dots + bias)
        coef = (-scale * sgn) / (1.0 + jnp.exp(-arg))
        return arg, coef.astype(bf16)

    gid_own = jnp.where(own_col >= 0.0, own_col + (b * 128).astype(f32), -1.0)
    dtext = jnp.zeros((CAPS, E), f32)
    for c in range(4):
        chunk = img[c].reshape(512, E)
        _, coef = pair(mm_nt(text, chunk), gid_own, c * 512)
        dtext = dtext + mm(coef, chunk)
    dproj = (
        scale_inv * (dtext - text_unit * jnp.sum(text_unit * dtext, axis=1, keepdims=True))
    ).astype(bf16)
    live = jnp.where(own_col >= 0.0, rcount, 0.0)

    def dcap_tile(i, _):
        rows = pl.ds(pl.multiple_of(i * TN, TN), TN)
        dpool = mm_nt(dproj, headv[rows, :]).astype(bf16).astype(f32)
        dc = (dpool * live).astype(bf16)
        dcap[:, rows] = dc
        stack[0:CAPS, rows] = dc
        return 0

    lax.fori_loop(0, DT // TN, dcap_tile, 0)

    def dnorm_tile(i, _):
        rows = pl.ds(pl.multiple_of(i * TN, TN), TN)
        dn = mm_nt(dcap[...], wv[rows, :])
        gsrc[:, rows] = jnp.sum(xp[:, rows] * dn, axis=0, keepdims=True)
        hi, lo = split2(dn * gain_ref[:, rows])
        stack[CAPS : 2 * CAPS, rows] = hi
        stack[2 * CAPS : 3 * CAPS, rows] = hi
        stack[3 * CAPS : 4 * CAPS, rows] = lo
        return 0

    lax.fori_loop(0, DT // TN, dnorm_tile, 0)

    for r in range(16):
        gbuf[d, r : r + 1, :] = gsrc[:, r * 128 : (r + 1) * 128]

    def dp_copy(buf, src, idx, k, ssem, rsem):
        return pltpu.make_async_remote_copy(
            src_ref=src, dst_ref=buf.at[idx], send_sem=ssem.at[k], recv_sem=rsem.at[k],
            device_id=(b, (d + k + 1) % ND), device_id_type=MESH,
        )

    for k in range(ND - 1):
        cp = dp_copy(gbuf, gbuf.at[d], d, k, g_send, g_recv)
        cp.start()
        sends.append(cp)

    for k in range(7):
        frm = text_peer(k, -1)
        text_core(k, frm + 1 - 2 * core).wait_recv()
    text_core(7, sib[0]).wait_recv()
    for k in range(NB - 1):
        frm = (b + NB - 1 - k) % NB
        pltpu.make_async_remote_copy(
            src_ref=arcv.at[frm], dst_ref=arcv.at[frm], send_sem=a_send.at[k], recv_sem=a_recv.at[k],
            device_id=(frm, d), device_id_type=MESH,
        ).wait_recv()

    slots = NB * CAPS
    owner = tbuf[:, :, E:PW].reshape(slots, 128).astype(f32)[:, 0:1]
    block = (iota((slots, 1), 0) // CAPS * 128).astype(f32)
    gid = jnp.where(owner >= 0.0, owner + block, -1.0)
    share = arcv[...].reshape(slots, 128).astype(f32)
    share_t = share.T.astype(bf16)
    bacc[...] = jnp.zeros((128, E), f32)
    rsacc[...] = jnp.zeros((slots, 1), f32)

    def pair_chunk(c, _):
        chunk = img[c].reshape(512, E)
        dots = mm_nt(tbuf[:, :, 0:E].reshape(slots, E), chunk)
        _, coef = pair(dots, gid, c * 512)
        rsacc[...] += jnp.sum(coef.astype(f32) * dots, axis=1, keepdims=True)
        zt = mm(share_t, coef).astype(bf16)
        bacc[...] += mm(zt, chunk)
        return 0

    lax.fori_loop(0, 4, pair_chunk, 0)

    texts = tbuf[:, :, 0:E].reshape(slots, E)
    minus_t = (share * rsacc[...]).T.astype(bf16)
    bpart = bacc[...] - mm(minus_t, texts)
    group = img[z, xh, core].reshape(128, E)
    arg, coef = pair(mm_nt(texts, group), gid, b * 128)
    soft = jnp.maximum(arg, 0.0) + jnp.log1p(jnp.exp(-jnp.abs(arg)))
    lrow_part = jnp.sum(jnp.where(gid >= 0.0, soft, 0.0), axis=0, keepdims=True)
    dimg_part = mm(coef.astype(f32).T.astype(bf16), texts)
    c3s[:, :, 0:E] = dimg_part.reshape(ND, 16, E).astype(bf16)
    c3s[:, :, E : 2 * E] = bpart.reshape(ND, 16, E).astype(bf16)
    c3r[d] = c3s[d]
    lbuf[d] = jnp.broadcast_to(lrow_part, (8, 128))
    for k in range(ND - 1):
        cp = dp_copy(c3r, c3s.at[(d + k + 1) % ND], d, k, c_send, c_recv)
        cp.start()
        sends.append(cp)
        cp = dp_copy(lbuf, lbuf.at[d], d, k, l_send, l_recv)
        cp.start()
        sends.append(cp)

    for k in range(ND - 1):
        frm = (d + ND - 1 - k) % ND
        dp_copy(gbuf, gbuf.at[frm], frm, k, g_send, g_recv).wait_recv()
    g2[b] = jnp.sum(gbuf[...], axis=0)
    for k in range(NB - 1):
        cp = pltpu.make_async_remote_copy(
            src_ref=g2.at[b], dst_ref=g2.at[b], send_sem=h_send.at[k], recv_sem=h_recv.at[k],
            device_id=((b + k + 1) % NB, d), device_id_type=MESH,
        )
        cp.start()
        sends.append(cp)

    stores = []
    for i in range(4):
        rows = pl.ds(i * 128, 128)
        xb = tok[rows, :]
        lc = lcol[rows, :]
        q = mm_nt(xb, stack[...])
        mine = (segt[rows, :] == cap_of) & ((kind == 1) | (kind == 3))
        mean = jnp.sum(jnp.where(mine, q, 0.0), axis=1, keepdims=True) * (1.0 / DT)
        inv = invc[rows, :]
        drop = inv * inv * inv * mean
        full = mm(lc.astype(bf16), stack[...])
        stage[rows, :] = (full - xb.astype(f32) * drop).astype(bf16)
        cp = pltpu.make_async_copy(stage.at[rows, :], dtok_hbm.at[rows, :], st_sem.at[i])
        cp.start()
        stores.append(cp)

    for k in range(ND - 1):
        frm = (d + ND - 1 - k) % ND
        dp_copy(c3r, c3r.at[frm], frm, k, c_send, c_recv).wait_recv()
        dp_copy(lbuf, lbuf.at[frm], frm, k, l_send, l_recv).wait_recv()
    dimg = jnp.sum(c3r[:, :, 0:E].astype(f32), axis=0)
    bmine = jnp.sum(c3r[:, :, E : 2 * E].astype(f32), axis=0)
    dimg_out[...] = img_inv * (dimg - img_unit * jnp.sum(img_unit * dimg, axis=1, keepdims=True))
    hi, lo = split2(bmine)
    both = jnp.concatenate([hi, lo], axis=0)

    def dw_tile(i, _):
        rows = pl.ds(pl.multiple_of(i * TN, TN), TN)
        dw = mm_nt(both, headv[rows, :])
        dw_out[:, rows] = dw[0:16] + dw[16:32]
        return 0

    lax.fori_loop(0, DT // TN, dw_tile, 0)

    lsum = jnp.sum(lbuf[...], axis=0)[0:1] * (1.0 / TOTAL)
    col = jnp.sum(
        jnp.where(iota((16, 128), 1) == iota((16, 128), 0) + 16 * d, jnp.broadcast_to(lsum, (16, 128)), 0.0),
        axis=1,
        keepdims=True,
    )
    loss_out[...] = jnp.sum(jnp.where(iota((16, 16), 0) == iota((16, 16), 1), col, 0.0), axis=0, keepdims=True)

    for k in range(NB - 1):
        frm = (b + NB - 1 - k) % NB
        pltpu.make_async_remote_copy(
            src_ref=g2.at[frm], dst_ref=g2.at[frm], send_sem=h_send.at[k], recv_sem=h_recv.at[k],
            device_id=(frm, d), device_id_type=MESH,
        ).wait_recv()
    dgain_out[...] = jnp.sum(g2[...], axis=0)

    for cp in stores:
        cp.wait()
    for cp in sends:
        cp.wait_send()


def per_device(tokens, segment_ids, owners, images, weight, gain, head, logit_params):
    vmem = pl.BlockSpec(memory_space=pltpu.VMEM)
    hbm = pl.BlockSpec(memory_space=pl.ANY)
    dma = pltpu.SemaphoreType.DMA
    loss, d_tokens, d_weight, d_gain, d_images = pl.pallas_call(
        kernel,
        out_shape=(
            jax.ShapeDtypeStruct((1, 16), f32),
            jax.ShapeDtypeStruct((ROWS, DT), bf16),
            jax.ShapeDtypeStruct((16, DT), f32),
            jax.ShapeDtypeStruct((16, 128), f32),
            jax.ShapeDtypeStruct((16, E), f32),
        ),
        in_specs=[hbm, hbm, hbm, vmem, vmem, vmem, vmem, pl.BlockSpec(memory_space=pltpu.SMEM)],
        out_specs=(vmem, hbm, vmem, vmem, vmem),
        scratch_shapes=[
            pltpu.VMEM((ROWS, DT), bf16),
            pltpu.VMEM((DT, DT), bf16),
            pltpu.VMEM((DT, E), bf16),
            pltpu.VMEM((4, 2, 2, 4, 2, 16, E), bf16),
            pltpu.VMEM((ROWS, 128), f32),
            pltpu.VMEM((ROWS, 128), f32),
            pltpu.VMEM((ROWS, 1), f32),
            pltpu.VMEM((CAPS, DT), f32),
            pltpu.VMEM((CAPS, DT), f32),
            pltpu.VMEM((2 * CAPS, DT), bf16),
            pltpu.VMEM((CAPS, DT), bf16),
            pltpu.VMEM((NB, CAPS, 128), bf16),
            pltpu.VMEM((NB, CAPS, 128), bf16),
            pltpu.VMEM((NB, CAPS, PW), bf16),
            pltpu.VMEM((CAPS, DT), bf16),
            pltpu.VMEM((4 * CAPS, DT), bf16),
            pltpu.VMEM((ROWS, DT), bf16),
            pltpu.VMEM((128, E), f32),
            pltpu.VMEM((NB * CAPS, 1), f32),
            pltpu.VMEM((ND, 16, 2 * E), bf16),
            pltpu.VMEM((ND, 16, 2 * E), bf16),
            pltpu.VMEM((ND, 8, 128), f32),
            pltpu.VMEM((1, DT), f32),
            pltpu.VMEM((ND, 16, 128), f32),
            pltpu.VMEM((NB, 16, 128), f32),
            dma((5,)),
            dma((DT // TN,)),
            dma((4,)),
            dma((PARTS, 3, 3)),
            dma((PARTS, 3, 3)),
            dma((PARTS, 4)),
            dma((PARTS, 4)),
            dma((7,)),
            dma((7,)),
            dma((8,)),
            dma((8,)),
            dma((NB - 1,)),
            dma((NB - 1,)),
            dma((ND - 1,)),
            dma((ND - 1,)),
            dma((ND - 1,)),
            dma((ND - 1,)),
            dma((ND - 1,)),
            dma((ND - 1,)),
            dma((NB - 1,)),
            dma((NB - 1,)),
        ],
        compiler_params=pltpu.CompilerParams(
            collective_id=0, has_side_effects=True, vmem_limit_bytes=56 * 1024 * 1024
        ),
    )(tokens, weight, head, segment_ids, owners, images, gain.reshape(1, DT), logit_params)
    return loss.reshape(16), d_tokens, d_weight, d_gain.reshape(DT), d_images


def solution(mesh):
    rows = P(("blk", "dp"), None)
    return jax.shard_map(
        per_device,
        mesh=mesh,
        in_specs=(rows, rows, rows, rows, P(), P(), P(), P()),
        out_specs=(P(("blk", "dp")), rows, rows, P(), rows),
        check_vma=False,
    )
```

```python
import functools

import jax
import jax.numpy as jnp
from jax import lax
from jax.experimental import pallas as pl
from jax.experimental.pallas import tpu as pltpu
from jax.sharding import PartitionSpec as P

f32 = jnp.float32
bf16 = jnp.bfloat16
MESH = pl.DeviceIdType.MESH

DT = 2048
E = 1152
ROWS = 512
CAPS = 32
NB = 16
ND = 8
TOTAL = 2048
PW = E + 128
PARTS = 3
ORDERS = (("x", "y", "z"), ("y", "z", "x"), ("z", "x", "y"))
COLUMNS = ((0, 256), (256, 256), (512, 640))
TN = 512
UNROLL = True


def mm(a, b):
    return lax.dot_general(a, b, (((1,), (0,)), ((), ())), preferred_element_type=f32)


def mm_nt(a, b):
    return lax.dot_general(a, b, (((1,), (1,)), ((), ())), preferred_element_type=f32)


def split2(v):
    hi = v.astype(bf16)
    return hi, (v - hi.astype(f32)).astype(bf16)


def iota(shape, dim):
    return lax.broadcasted_iota(jnp.int32, shape, dim)


def kernel(
    tok_hbm, w_hbm, head_hbm, seg_hbm, own_hbm, img_hbm, gain_hbm, lp_ref,
    loss_out, dtok_hbm, dw_out, dgain_out, dimg_out,
    tok, wv, headv, img, lcol, segt, invc, xs, xp, npst, pooled, asrc, arcv, tbuf, dcap, stack,
    seg_ref, own_ref, img_ref, gain_ref, stage, wh, coefs, zc, bacc, rsacc, c3as, c3ar, c3bs, c3br, gbuf, g2,
    ld_sem, w_sem, in_sem, st_sem,
    i_send, i_recv, j_send, j_recv, ic_send, ic_recv, t_send, t_recv, tc_send, tc_recv, a_send, a_recv,
    ca_send, ca_recv, cb_send, cb_recv, g_send, g_recv, h_send, h_recv,
):
    b = lax.axis_index("blk")
    d = lax.axis_index("dp")
    z, xh, core = b // 4, (b // 2) % 2, b % 2
    y, xl = d // 2, d % 2
    x = xh * 2 + xl
    sib = (b + 1 - 2 * core, d)

    here = {"x": x, "y": y, "z": z, "core": core}

    def device(at):
        return (at["z"] * 4 + (at["x"] // 2) * 2 + at["core"], at["y"] * 2 + at["x"] % 2)

    def step_of(axis, n):
        at = dict(here)
        at[axis] = (here[axis] + 4 + n) % 4
        return at

    barrier = pltpu.get_barrier_semaphore()
    pl.semaphore_signal(barrier, inc=1, device_id=sib, device_id_type=MESH)
    for axis in ("x", "y", "z"):
        for k in (1, 3, 2):
            pl.semaphore_signal(barrier, inc=1, device_id=device(step_of(axis, k)), device_id_type=MESH)

    inputs = []
    for i, (src, dst) in enumerate(((img_hbm, img_ref), (seg_hbm, seg_ref), (own_hbm, own_ref), (gain_hbm, gain_ref))):
        cp = pltpu.make_async_copy(src, dst, in_sem.at[i])
        cp.start()
        inputs.append(cp)
    loads = []
    for i in range(4):
        cp = pltpu.make_async_copy(
            tok_hbm.at[pl.ds(i * 128, 128), :], tok.at[pl.ds(i * 128, 128), :], ld_sem.at[i]
        )
        cp.start()
        loads.append(cp)
    wloads = []
    for i in range(DT // TN):
        cp = pltpu.make_async_copy(
            w_hbm.at[:, pl.ds(i * TN, TN)], wv.at[:, pl.ds(i * TN, TN)], w_sem.at[i]
        )
        cp.start()
        wloads.append(cp)
    hload = pltpu.make_async_copy(head_hbm, headv, ld_sem.at[4])
    hload.start()

    inputs[0].wait()
    im = img_ref[...].astype(f32)
    img_inv = lax.rsqrt(jnp.sum(im * im, axis=1, keepdims=True) + 1e-06)
    img_unit = im * img_inv
    img[z, xh, core, y, xl] = img_unit.astype(bf16)

    sends = []

    def region(p, at):
        def pick(name):
            return slice(None) if at[name] is None else at[name]

        xx = at["x"]
        return img.at[
            pick("z"),
            slice(None) if xx is None else xx // 2,
            at["core"],
            pick("y"),
            slice(None) if xx is None else xx % 2,
            :,
            pl.ds(*COLUMNS[p]),
        ]

    def ring_region(p, done, where):
        at = dict(where)
        for name in done:
            at[name] = None
        return region(p, at)

    def ring_copy(p, s, k, where, to):
        ref = ring_region(p, ORDERS[p][:s], where)
        return pltpu.make_async_remote_copy(
            src_ref=ref, dst_ref=ref, send_sem=i_send.at[p, s, k], recv_sem=i_recv.at[p, s, k],
            device_id=device(to), device_id_type=MESH,
        )

    def last_copy(p, j, k, where, to):
        first, second, _ = ORDERS[p]
        at = dict(where)
        at[second] = (here[second] + 4 - j) % 4
        ref = ring_region(p, (first,), at)
        return pltpu.make_async_remote_copy(
            src_ref=ref, dst_ref=ref, send_sem=j_send.at[p, j, k], recv_sem=j_recv.at[p, j, k],
            device_id=device(to), device_id_type=MESH,
        )

    def ring_send(p, s):
        for k in range(3):
            cp = ring_copy(p, s, k, here, step_of(ORDERS[p][s], k + 1))
            cp.start()
            sends.append(cp)

    def ring_wait(p, s, k):
        frm = step_of(ORDERS[p][s], -1 - k)
        ring_copy(p, s, k, frm, frm).wait_recv()

    def last_send(p, j):
        for k in range(3):
            cp = last_copy(p, j, k, here, step_of(ORDERS[p][2], k + 1))
            cp.start()
            sends.append(cp)

    def last_wait(p, k):
        frm = step_of(ORDERS[p][2], -1 - k)
        for j in range(4):
            last_copy(p, j, k, frm, frm).wait_recv()

    def core_copy(p, q, own):
        order = ORDERS[p]
        at = dict(here)
        for name in order[:2]:
            at[name] = None
        if q:
            at[order[2]] = (here[order[2]] + 4 - q) % 4
        if not own:
            at["core"] = 1 - core
        ref = region(p, at)
        return pltpu.make_async_remote_copy(
            src_ref=ref, dst_ref=ref, send_sem=ic_send.at[p, q], recv_sem=ic_recv.at[p, q],
            device_id=sib, device_id_type=MESH,
        )

    def core_send(p, q):
        cp = core_copy(p, q, True)
        cp.start()
        sends.append(cp)

    pl.semaphore_wait(barrier, 10)
    for p in range(PARTS):
        ring_send(p, 0)

    for cp in inputs[1:]:
        cp.wait()
    segf = seg_ref[...].astype(f32)
    segt[...] = jnp.broadcast_to(segf, (128, ROWS)).T
    lane = iota((128, 128), 1)
    cap_of = (lane % CAPS).astype(f32)
    kind = lane // CAPS

    def token_rows(i):
        loads[i].wait()
        rows = pl.ds(i * 128, 128)
        xx = tok[rows, :].astype(f32)
        inv = lax.rsqrt(jnp.sum(xx * xx, axis=1, keepdims=True) * (1.0 / DT) + 1e-06)
        invc[rows, :] = inv
        hi = inv.astype(bf16).astype(f32)
        lo = inv - hi
        val = jnp.where(kind == 0, 1.0, jnp.where(kind == 2, lo, hi))
        lcol[rows, :] = jnp.where(segt[rows, :] == cap_of, val, 0.0)

    for i in range(4):
        token_rows(i)

    lrow = lcol[...].T.astype(bf16)

    def pool_tile(i, _):
        cols = pl.ds(pl.multiple_of(i * TN, TN), TN)
        acc = mm(lrow, tok[:, cols])
        xs[:, cols] = acc[0:CAPS]
        xpt = acc[CAPS : 2 * CAPS] + acc[2 * CAPS : 3 * CAPS]
        xp[:, cols] = xpt
        hi, lo = split2(xpt * gain_ref[:, cols])
        npst[0:CAPS, cols] = hi
        npst[CAPS : 2 * CAPS, cols] = lo
        return 0

    lax.fori_loop(0, DT // TN, pool_tile, 0)

    sel = (jnp.broadcast_to(segf, (CAPS, ROWS)) == iota((CAPS, ROWS), 0).astype(f32)).astype(f32)
    rcount = 1.0 / jnp.maximum(jnp.sum(sel, axis=1, keepdims=True), 1.0)
    ownf = own_ref[...].astype(f32)
    own_col = jnp.sum(
        jnp.where(iota((CAPS, CAPS), 0) == iota((CAPS, CAPS), 1), jnp.broadcast_to(ownf, (CAPS, CAPS)), 0.0),
        axis=1,
        keepdims=True,
    )

    for i in range(DT // TN):
        if i == 2:
            for p in range(PARTS):
                for k in range(3):
                    ring_wait(p, 0, k)
                ring_send(p, 1)
                last_send(p, 0)
        wloads[i].wait()
        cols = pl.ds(i * TN, TN)
        yy = mm(npst[...], wv[:, cols])
        pooled[:, cols] = ((xs[:, cols] + yy[0:CAPS] + yy[CAPS : 2 * CAPS]) * rcount).astype(bf16)

    hload.wait()
    proj = mm(pooled[...], headv[...])
    scale_inv = lax.rsqrt(jnp.sum(proj * proj, axis=1, keepdims=True) + 1e-06)
    text_unit = proj * scale_inv
    text = text_unit.astype(bf16)
    tbuf[b, :, 0:E] = text
    tbuf[b, :, E:PW] = jnp.broadcast_to(own_col, (CAPS, 128)).astype(bf16)
    factor = scale_inv * rcount
    for j in range(NB):
        cols = pl.ds(j * 128, 128)
        asrc[j] = (xp[:, cols] * factor).astype(bf16)
    arcv[b] = asrc[b]

    def text_peer(k, sign):
        dz, dx = (k + 1) // 2, (k + 1) % 2
        return ((z + 4 + sign * dz) % 4) * 4 + ((xh + dx) % 2) * 2 + core

    def text_copy(k, idx, to):
        return pltpu.make_async_remote_copy(
            src_ref=tbuf.at[idx], dst_ref=tbuf.at[idx], send_sem=t_send.at[k], recv_sem=t_recv.at[k],
            device_id=(to, d), device_id_type=MESH,
        )

    def text_core(k, idx):
        return pltpu.make_async_remote_copy(
            src_ref=tbuf.at[idx], dst_ref=tbuf.at[idx], send_sem=tc_send.at[k], recv_sem=tc_recv.at[k],
            device_id=sib, device_id_type=MESH,
        )

    for k in range(7):
        cp = text_copy(k, b, text_peer(k, 1))
        cp.start()
        sends.append(cp)
    cp = text_core(7, b)
    cp.start()
    sends.append(cp)
    wh[...] = mm(wv[pl.ds(pl.multiple_of(b * 128, 128), 128), :], headv[...])

    for k in (0, 2, 1):
        for p in range(PARTS):
            ring_wait(p, 1, k)
            last_send(p, k + 1)
    for p in range(PARTS):
        core_send(p, 0)
    for k in range(NB - 1):
        to = (b + k + 1) % NB
        cp = pltpu.make_async_remote_copy(
            src_ref=asrc.at[to], dst_ref=arcv.at[b], send_sem=a_send.at[k], recv_sem=a_recv.at[k],
            device_id=(to, d), device_id_type=MESH,
        )
        cp.start()
        sends.append(cp)
    for k in range(7):
        frm = text_peer(k, -1)
        text_copy(k, frm, frm).wait_recv()
        cp = text_core(k, frm)
        cp.start()
        sends.append(cp)
    for k in (0, 2, 1):
        for p in range(PARTS):
            last_wait(p, k)
            core_send(p, k + 1)
    for p in range(PARTS):
        for q in range(4):
            core_copy(p, q, False).wait_recv()

    scale = jnp.exp(jnp.full((1, 128), lp_ref[0], f32))[:, 0:1]
    bias = jnp.full((1, 128), lp_ref[1], f32)[:, 0:1]

    def pair(dots, gid, first):
        ids = (iota((1, dots.shape[1]), 1) + first).astype(f32)
        val = scale * dots + bias
        same = gid == ids
        arg = jnp.where(same, -val, val)
        coef = jnp.where(same, -scale, scale) * pl.reciprocal(1.0 + jnp.exp(-arg), approx=True)
        return arg, coef

    def dp_copy(buf, src, idx, k, ssem, rsem):
        return pltpu.make_async_remote_copy(
            src_ref=src, dst_ref=buf.at[idx], send_sem=ssem.at[k], recv_sem=rsem.at[k],
            device_id=(b, (d + k + 1) % ND), device_id_type=MESH,
        )

    def dp_wait(buf, k, ssem, rsem):
        frm = (d + ND - 1 - k) % ND
        dp_copy(buf, buf.at[frm], frm, k, ssem, rsem).wait_recv()

    for k in range(7):
        frm = text_peer(k, -1)
        text_core(k, frm + 1 - 2 * core).wait_recv()
    text_core(7, sib[0]).wait_recv()

    slots = NB * CAPS
    owner = tbuf[:, :, E:PW].reshape(slots, 128).astype(f32)[:, 0:1]
    block = (iota((slots, 1), 0) // CAPS * 128).astype(f32)
    gid = jnp.where(owner >= 0.0, owner + block, -1.0)
    texts = tbuf[:, :, 0:E].reshape(slots, E)
    group = img[z, xh, core].reshape(128, E)
    arg, coef = pair(mm_nt(texts, group), gid, b * 128)
    dimg_part = mm(coef.T.astype(bf16), texts)
    c3as[...] = dimg_part.reshape(ND, 16, E).astype(bf16)
    c3ar[d] = c3as[d]
    for k in range(ND - 1):
        cp = dp_copy(c3ar, c3as.at[(d + k + 1) % ND], d, k, ca_send, ca_recv)
        cp.start()
        sends.append(cp)
    soft = jnp.maximum(arg, 0.0) + jnp.log1p(jnp.exp(-jnp.abs(arg)))
    loss_part = jnp.sum(jnp.where(gid >= 0.0, soft, 0.0), axis=0, keepdims=True)

    for k in range(NB - 1):
        frm = (b + NB - 1 - k) % NB
        pltpu.make_async_remote_copy(
            src_ref=arcv.at[frm], dst_ref=arcv.at[frm], send_sem=a_send.at[k], recv_sem=a_recv.at[k],
            device_id=(frm, d), device_id_type=MESH,
        ).wait_recv()
    share = arcv[...].reshape(slots, 128).astype(f32)
    share_t = share.T.astype(bf16)
    bacc[...] = jnp.zeros((128 + CAPS, E), f32)
    rsacc[...] = jnp.zeros((slots, 1), f32)

    def pair_chunk(c, _):
        chunk = img[c].reshape(512, E)
        dots = mm_nt(tbuf[:, :, 0:E].reshape(slots, E), chunk)
        _, coef = pair(dots, gid, c * 512)
        rsacc[...] += jnp.sum(coef * dots, axis=1, keepdims=True)
        coefs[...] = coef.astype(bf16)
        zc[0:128, :] = mm(share_t, coefs[...]).astype(bf16)
        zc[128 : 128 + CAPS, :] = coefs[pl.ds(pl.multiple_of(b * CAPS, CAPS), CAPS), :]
        bacc[...] += mm(zc[...], chunk)
        return 0

    lax.fori_loop(0, 4, pair_chunk, 0, unroll=UNROLL)

    minus_t = (share * rsacc[...]).T.astype(bf16)
    bpart = bacc[0:128, :] - mm(minus_t, texts)
    c3bs[...] = bpart.reshape(ND, 16, E).astype(bf16)
    c3br[d] = c3bs[d]
    gain_part = jnp.sum(bpart * wh[...], axis=1, keepdims=True)
    gbuf[d, 0:8, :] = jnp.broadcast_to(loss_part, (8, 128))
    gbuf[d, 8:16, :] = jnp.broadcast_to(gain_part, (128, 128)).T[0:8]
    for k in range(ND - 1):
        cp = dp_copy(gbuf, gbuf.at[d], d, k, g_send, g_recv)
        cp.start()
        sends.append(cp)
    for k in range(ND - 1):
        cp = dp_copy(c3br, c3bs.at[(d + k + 1) % ND], d, k, cb_send, cb_recv)
        cp.start()
        sends.append(cp)

    dtext = bacc[128 : 128 + CAPS, :]
    dproj = (
        scale_inv * (dtext - text_unit * jnp.sum(text_unit * dtext, axis=1, keepdims=True))
    ).astype(bf16)
    live = jnp.where(own_col >= 0.0, rcount, 0.0)

    def dcap_tile(i, _):
        rows = pl.ds(pl.multiple_of(i * TN, TN), TN)
        dpool = mm_nt(dproj, headv[rows, :]).astype(bf16).astype(f32)
        dc = (dpool * live).astype(bf16)
        dcap[:, rows] = dc
        stack[0:CAPS, rows] = dc
        return 0

    lax.fori_loop(0, DT // TN, dcap_tile, 0)

    for k in range(ND - 1):
        dp_wait(gbuf, k, g_send, g_recv)
    gsum = jnp.sum(gbuf[...], axis=0)
    g2[b] = gsum[8:16]
    for k in range(NB - 1):
        cp = pltpu.make_async_remote_copy(
            src_ref=g2.at[b], dst_ref=g2.at[b], send_sem=h_send.at[k], recv_sem=h_recv.at[k],
            device_id=((b + k + 1) % NB, d), device_id_type=MESH,
        )
        cp.start()
        sends.append(cp)

    def dnorm_tile(i, _):
        rows = pl.ds(pl.multiple_of(i * TN, TN), TN)
        hi, lo = split2(mm_nt(dcap[...], wv[rows, :]) * gain_ref[:, rows])
        stack[CAPS : 2 * CAPS, rows] = hi
        stack[2 * CAPS : 3 * CAPS, rows] = hi
        stack[3 * CAPS : 4 * CAPS, rows] = lo
        return 0

    lax.fori_loop(0, DT // TN, dnorm_tile, 0)

    stores = []
    for i in range(4):
        rows = pl.ds(i * 128, 128)
        xb = tok[rows, :]
        lc = lcol[rows, :]
        q = mm_nt(xb, stack[...])
        mine = (segt[rows, :] == cap_of) & ((kind == 1) | (kind == 3))
        mean = jnp.sum(jnp.where(mine, q, 0.0), axis=1, keepdims=True) * (1.0 / DT)
        inv = invc[rows, :]
        drop = inv * inv * inv * mean
        full = mm(lc.astype(bf16), stack[...])
        stage[rows, :] = (full - xb.astype(f32) * drop).astype(bf16)
        cp = pltpu.make_async_copy(stage.at[rows, :], dtok_hbm.at[rows, :], st_sem.at[i])
        cp.start()
        stores.append(cp)

    for k in range(ND - 1):
        dp_wait(c3ar, k, ca_send, ca_recv)
    dimg = jnp.sum(c3ar[...].astype(f32), axis=0)
    dimg_out[...] = img_inv * (dimg - img_unit * jnp.sum(img_unit * dimg, axis=1, keepdims=True))
    for k in range(ND - 1):
        dp_wait(c3br, k, cb_send, cb_recv)
    mine = iota((16, 128), 1) == iota((16, 128), 0) + 16 * d

    def own_rows(row):
        return jnp.sum(jnp.where(mine, jnp.broadcast_to(row, (16, 128)), 0.0), axis=1, keepdims=True)

    gain_col = own_rows(gain_ref[:, pl.ds(pl.multiple_of(b * 128, 128), 128)])
    hi, lo = split2(jnp.sum(c3br[...].astype(f32), axis=0) * gain_col)
    both = jnp.concatenate([hi, lo], axis=0)

    def dw_tile(i, _):
        rows = pl.ds(pl.multiple_of(i * TN, TN), TN)
        dw = mm_nt(both, headv[rows, :])
        dw_out[:, rows] = dw[0:16] + dw[16:32]
        return 0

    lax.fori_loop(0, DT // TN, dw_tile, 0)

    col = own_rows(gsum[0:1] * (1.0 / TOTAL))
    loss_out[...] = jnp.sum(jnp.where(iota((16, 16), 0) == iota((16, 16), 1), col, 0.0), axis=0, keepdims=True)

    for k in range(NB - 1):
        frm = (b + NB - 1 - k) % NB
        pltpu.make_async_remote_copy(
            src_ref=g2.at[frm], dst_ref=g2.at[frm], send_sem=h_send.at[k], recv_sem=h_recv.at[k],
            device_id=(frm, d), device_id_type=MESH,
        ).wait_recv()
    for r in range(NB):
        dgain_out[r : r + 1, :] = g2[r, 0:1, :]

    for cp in stores:
        cp.wait()
    for cp in sends:
        cp.wait_send()


def hand_over(loss, dtok, dw, dgain, dimg, loss_out, dtok_out, dw_out, dgain_out, dimg_out, buf, ins, outs):
    reads = []
    for i in range(4):
        cp = pltpu.make_async_copy(dtok.at[pl.ds(i * 128, 128), :], buf.at[pl.ds(i * 128, 128), :], ins.at[i])
        cp.start()
        reads.append(cp)
    loss_out[...] = loss[...]
    dw_out[...] = dw[...]
    dgain_out[...] = dgain[...]
    dimg_out[...] = dimg[...]
    writes = []
    for i in range(4):
        reads[i].wait()
        cp = pltpu.make_async_copy(buf.at[pl.ds(i * 128, 128), :], dtok_out.at[pl.ds(i * 128, 128), :], outs.at[i])
        cp.start()
        writes.append(cp)
    for cp in writes:
        cp.wait()


def per_device(tokens, segment_ids, owners, images, weight, gain, head, logit_params):
    vmem = pl.BlockSpec(memory_space=pltpu.VMEM)
    hbm = pl.BlockSpec(memory_space=pl.ANY)
    dma = pltpu.SemaphoreType.DMA
    shapes = (
        jax.ShapeDtypeStruct((1, 16), f32),
        jax.ShapeDtypeStruct((ROWS, DT), bf16),
        jax.ShapeDtypeStruct((16, DT), f32),
        jax.ShapeDtypeStruct((16, 128), f32),
        jax.ShapeDtypeStruct((16, E), f32),
    )
    held = pl.pallas_call(
        kernel,
        out_shape=shapes,
        in_specs=[hbm, hbm, hbm, hbm, hbm, hbm, hbm, pl.BlockSpec(memory_space=pltpu.SMEM)],
        out_specs=(vmem, hbm, vmem, vmem, vmem),
        scratch_shapes=[
            pltpu.VMEM((ROWS, DT), bf16),
            pltpu.VMEM((DT, DT), bf16),
            pltpu.VMEM((DT, E), bf16),
            pltpu.VMEM((4, 2, 2, 4, 2, 16, E), bf16),
            pltpu.VMEM((ROWS, 128), f32),
            pltpu.VMEM((ROWS, 128), f32),
            pltpu.VMEM((ROWS, 1), f32),
            pltpu.VMEM((CAPS, DT), f32),
            pltpu.VMEM((CAPS, DT), f32),
            pltpu.VMEM((2 * CAPS, DT), bf16),
            pltpu.VMEM((CAPS, DT), bf16),
            pltpu.VMEM((NB, CAPS, 128), bf16),
            pltpu.VMEM((NB, CAPS, 128), bf16),
            pltpu.VMEM((NB, CAPS, PW), bf16),
            pltpu.VMEM((CAPS, DT), bf16),
            pltpu.VMEM((4 * CAPS, DT), bf16),
            pltpu.VMEM((1, ROWS), jnp.int32),
            pltpu.VMEM((1, CAPS), jnp.int32),
            pltpu.VMEM((16, E), bf16),
            pltpu.VMEM((1, DT), f32),
            pltpu.VMEM((ROWS, DT), bf16),
            pltpu.VMEM((128, E), f32),
            pltpu.VMEM((NB * CAPS, 512), bf16),
            pltpu.VMEM((128 + CAPS, 512), bf16),
            pltpu.VMEM((128 + CAPS, E), f32),
            pltpu.VMEM((NB * CAPS, 1), f32),
            pltpu.VMEM((ND, 16, E), bf16),
            pltpu.VMEM((ND, 16, E), bf16),
            pltpu.VMEM((ND, 16, E), bf16),
            pltpu.VMEM((ND, 16, E), bf16),
            pltpu.VMEM((ND, 16, 128), f32),
            pltpu.VMEM((NB, 8, 128), f32),
            dma((5,)),
            dma((DT // TN,)),
            dma((4,)),
            dma((4,)),
            dma((PARTS, 2, 3)),
            dma((PARTS, 2, 3)),
            dma((PARTS, 4, 3)),
            dma((PARTS, 4, 3)),
            dma((PARTS, 4)),
            dma((PARTS, 4)),
            dma((7,)),
            dma((7,)),
            dma((8,)),
            dma((8,)),
            dma((NB - 1,)),
            dma((NB - 1,)),
            dma((ND - 1,)),
            dma((ND - 1,)),
            dma((ND - 1,)),
            dma((ND - 1,)),
            dma((ND - 1,)),
            dma((ND - 1,)),
            dma((NB - 1,)),
            dma((NB - 1,)),
        ],
        compiler_params=pltpu.CompilerParams(
            collective_id=0, has_side_effects=True, vmem_limit_bytes=56 * 1024 * 1024
        ),
    )(tokens, weight, head, segment_ids, owners, images, gain.reshape(1, DT), logit_params)
    loss, d_tokens, d_weight, d_gain, d_images = pl.pallas_call(
        hand_over,
        out_shape=shapes,
        in_specs=[vmem, hbm, vmem, vmem, vmem],
        out_specs=(vmem, hbm, vmem, vmem, vmem),
        scratch_shapes=[pltpu.VMEM((ROWS, DT), bf16), dma((4,)), dma((4,))],
        compiler_params=pltpu.CompilerParams(vmem_limit_bytes=56 * 1024 * 1024),
    )(*held)
    return loss.reshape(16), d_tokens, d_weight, d_gain.reshape(DT), d_images


def solution(mesh):
    rows = P(("blk", "dp"), None)
    return jax.shard_map(
        per_device,
        mesh=mesh,
        in_specs=(rows, rows, rows, rows, P(), P(), P(), P()),
        out_specs=(P(("blk", "dp")), rows, rows, P(), rows),
        check_vma=False,
    )
```

```python
import functools

import jax
import jax.numpy as jnp
from jax import lax
from jax.experimental import pallas as pl
from jax.experimental.pallas import tpu as pltpu
from jax.sharding import PartitionSpec as P

f32 = jnp.float32
bf16 = jnp.bfloat16
MESH = pl.DeviceIdType.MESH

DT = 2048
E = 1152
ROWS = 512
CAPS = 32
NB = 16
ND = 8
TOTAL = 2048
NC = 8
NR = 16
SLOTS = NC * CAPS
GR = NR * 16
PW = E + 128
PARTS = 3
ORDERS = (("x", "y", "z"), ("y", "z", "x"), ("z", "x", "y"))
COLUMNS = ((0, 256), (256, 384), (640, 512))
TN = 512
UNROLL = True


def mm(a, b):
    return lax.dot_general(a, b, (((1,), (0,)), ((), ())), preferred_element_type=f32)


def mm_nt(a, b):
    return lax.dot_general(a, b, (((1,), (1,)), ((), ())), preferred_element_type=f32)


def split2(v):
    hi = v.astype(bf16)
    return hi, (v - hi.astype(f32)).astype(bf16)


def iota(shape, dim):
    return lax.broadcasted_iota(jnp.int32, shape, dim)


def kernel(
    tok_hbm, w_hbm, head_hbm, seg_hbm, own_hbm, img_hbm, gain_hbm, lp_ref,
    loss_out, dtok_hbm, dw_out, dgain_out, dimg_out,
    tok, wv, headv, img, lcol, segt, invc, xs, xp, npst, pooled, asrc, arcv, tbuf, dcap, stack,
    seg_ref, own_ref, img_ref, gain_ref, stage, wh, coefs, zc, bacc, rsacc, c3as, c3ar, c3bs, c3br, gbuf, g2,
    ld_sem, w_sem, in_sem, st_sem,
    i_send, i_recv, j_send, j_recv, ic_send, ic_recv, t_send, t_recv, tc_send, tc_recv, a_send, a_recv,
    ca_send, ca_recv, cb_send, cb_recv, g_send, g_recv, h_send, h_recv,
):
    b = lax.axis_index("blk")
    d = lax.axis_index("dp")
    z, xh, core = b // 4, (b // 2) % 2, b % 2
    y, xl = d // 2, d % 2
    x = xh * 2 + xl
    sib = (b + 1 - 2 * core, d)
    place = z * 2 + core
    seat = xh * ND + d

    here = {"x": x, "y": y, "z": z, "core": core}

    def device(at):
        return (at["z"] * 4 + (at["x"] // 2) * 2 + at["core"], at["y"] * 2 + at["x"] % 2)

    def step_of(axis, n):
        at = dict(here)
        at[axis] = (here[axis] + 4 + n) % 4
        return at

    barrier = pltpu.get_barrier_semaphore()
    pl.semaphore_signal(barrier, inc=1, device_id=sib, device_id_type=MESH)
    for axis in ("x", "y", "z"):
        for k in (1, 3, 2):
            pl.semaphore_signal(barrier, inc=1, device_id=device(step_of(axis, k)), device_id_type=MESH)

    inputs = []
    for i, (src, dst) in enumerate(((img_hbm, img_ref), (seg_hbm, seg_ref), (own_hbm, own_ref), (gain_hbm, gain_ref))):
        cp = pltpu.make_async_copy(src, dst, in_sem.at[i])
        cp.start()
        inputs.append(cp)
    loads = []
    for i in range(4):
        cp = pltpu.make_async_copy(
            tok_hbm.at[pl.ds(i * 128, 128), :], tok.at[pl.ds(i * 128, 128), :], ld_sem.at[i]
        )
        cp.start()
        loads.append(cp)
    wloads = []
    for i in range(DT // TN):
        cp = pltpu.make_async_copy(
            w_hbm.at[:, pl.ds(i * TN, TN)], wv.at[:, pl.ds(i * TN, TN)], w_sem.at[i]
        )
        cp.start()
        wloads.append(cp)
    hload = pltpu.make_async_copy(head_hbm, headv, ld_sem.at[4])
    hload.start()

    inputs[0].wait()
    im = img_ref[...].astype(f32)
    img_inv = lax.rsqrt(jnp.sum(im * im, axis=1, keepdims=True) + 1e-06)
    img_unit = im * img_inv
    img[z, xh, core, y, xl] = img_unit.astype(bf16)

    sends = []

    def region(p, at):
        def pick(name):
            return slice(None) if at[name] is None else at[name]

        xx = at["x"]
        return img.at[
            pick("z"),
            slice(None) if xx is None else xx // 2,
            at["core"],
            pick("y"),
            slice(None) if xx is None else xx % 2,
            :,
            pl.ds(*COLUMNS[p]),
        ]

    def ring_region(p, done, where):
        at = dict(where)
        for name in done:
            at[name] = None
        return region(p, at)

    def ring_copy(p, s, k, where, to):
        ref = ring_region(p, ORDERS[p][:s], where)
        return pltpu.make_async_remote_copy(
            src_ref=ref, dst_ref=ref, send_sem=i_send.at[p, s, k], recv_sem=i_recv.at[p, s, k],
            device_id=device(to), device_id_type=MESH,
        )

    def last_copy(p, j, k, where, to):
        first, second, _ = ORDERS[p]
        at = dict(where)
        at[second] = (here[second] + 4 - j) % 4
        ref = ring_region(p, (first,), at)
        return pltpu.make_async_remote_copy(
            src_ref=ref, dst_ref=ref, send_sem=j_send.at[p, j, k], recv_sem=j_recv.at[p, j, k],
            device_id=device(to), device_id_type=MESH,
        )

    def ring_send(p, s):
        for k in range(3):
            cp = ring_copy(p, s, k, here, step_of(ORDERS[p][s], k + 1))
            cp.start()
            sends.append(cp)

    def ring_wait(p, s, k):
        frm = step_of(ORDERS[p][s], -1 - k)
        ring_copy(p, s, k, frm, frm).wait_recv()

    def last_send(p, j):
        for k in range(3):
            cp = last_copy(p, j, k, here, step_of(ORDERS[p][2], k + 1))
            cp.start()
            sends.append(cp)

    def last_wait(p, k):
        frm = step_of(ORDERS[p][2], -1 - k)
        for j in range(4):
            last_copy(p, j, k, frm, frm).wait_recv()

    def core_copy(p, q, own):
        order = ORDERS[p]
        at = dict(here)
        for name in order[:2]:
            at[name] = None
        if q:
            at[order[2]] = (here[order[2]] + 4 - q) % 4
        if not own:
            at["core"] = 1 - core
        ref = region(p, at)
        return pltpu.make_async_remote_copy(
            src_ref=ref, dst_ref=ref, send_sem=ic_send.at[p, q], recv_sem=ic_recv.at[p, q],
            device_id=sib, device_id_type=MESH,
        )

    def core_send(p, q):
        cp = core_copy(p, q, True)
        cp.start()
        sends.append(cp)

    pl.semaphore_wait(barrier, 10)
    for p in range(PARTS):
        ring_send(p, 0)

    for cp in inputs[1:]:
        cp.wait()
    segf = seg_ref[...].astype(f32)
    segt[...] = jnp.broadcast_to(segf, (128, ROWS)).T
    lane = iota((128, 128), 1)
    cap_of = (lane % CAPS).astype(f32)
    kind = lane // CAPS

    def token_rows(i):
        loads[i].wait()
        rows = pl.ds(i * 128, 128)
        xx = tok[rows, :].astype(f32)
        inv = lax.rsqrt(jnp.sum(xx * xx, axis=1, keepdims=True) * (1.0 / DT) + 1e-06)
        invc[rows, :] = inv
        hi = inv.astype(bf16).astype(f32)
        lo = inv - hi
        val = jnp.where(kind == 0, 1.0, jnp.where(kind == 2, lo, hi))
        lcol[rows, :] = jnp.where(segt[rows, :] == cap_of, val, 0.0)

    for i in range(4):
        token_rows(i)

    lrow = lcol[...].T.astype(bf16)

    def pool_tile(i, _):
        cols = pl.ds(pl.multiple_of(i * TN, TN), TN)
        acc = mm(lrow, tok[:, cols])
        xs[:, cols] = acc[0:CAPS]
        xpt = acc[CAPS : 2 * CAPS] + acc[2 * CAPS : 3 * CAPS]
        xp[:, cols] = xpt
        hi, lo = split2(xpt * gain_ref[:, cols])
        npst[0:CAPS, cols] = hi
        npst[CAPS : 2 * CAPS, cols] = lo
        return 0

    lax.fori_loop(0, DT // TN, pool_tile, 0)

    sel = (jnp.broadcast_to(segf, (CAPS, ROWS)) == iota((CAPS, ROWS), 0).astype(f32)).astype(f32)
    rcount = 1.0 / jnp.maximum(jnp.sum(sel, axis=1, keepdims=True), 1.0)
    ownf = own_ref[...].astype(f32)
    own_col = jnp.sum(
        jnp.where(iota((CAPS, CAPS), 0) == iota((CAPS, CAPS), 1), jnp.broadcast_to(ownf, (CAPS, CAPS)), 0.0),
        axis=1,
        keepdims=True,
    )

    for i in range(DT // TN):
        if i == 2:
            for p in range(PARTS):
                for k in range(3):
                    ring_wait(p, 0, k)
                ring_send(p, 1)
                last_send(p, 0)
        wloads[i].wait()
        cols = pl.ds(i * TN, TN)
        yy = mm(npst[...], wv[:, cols])
        pooled[:, cols] = ((xs[:, cols] + yy[0:CAPS] + yy[CAPS : 2 * CAPS]) * rcount).astype(bf16)

    hload.wait()
    proj = mm(pooled[...], headv[...])
    scale_inv = lax.rsqrt(jnp.sum(proj * proj, axis=1, keepdims=True) + 1e-06)
    text_unit = proj * scale_inv
    text = text_unit.astype(bf16)
    tbuf[place, :, 0:E] = text
    tbuf[place, :, E:PW] = jnp.broadcast_to(own_col, (CAPS, 128)).astype(bf16)
    factor = scale_inv * rcount
    for j in range(NB):
        cols = pl.ds(j * 128, 128)
        asrc[j // 4 * 2 + j % 2, j // 2 % 2] = (xp[:, cols] * factor).astype(bf16)
    arcv[place] = asrc[place]

    def text_copy(k, idx, to):
        return pltpu.make_async_remote_copy(
            src_ref=tbuf.at[idx], dst_ref=tbuf.at[idx], send_sem=t_send.at[k], recv_sem=t_recv.at[k],
            device_id=device(to), device_id_type=MESH,
        )

    def text_core(k, idx):
        return pltpu.make_async_remote_copy(
            src_ref=tbuf.at[idx], dst_ref=tbuf.at[idx], send_sem=tc_send.at[k], recv_sem=tc_recv.at[k],
            device_id=sib, device_id_type=MESH,
        )

    for k in range(3):
        cp = text_copy(k, place, step_of("z", k + 1))
        cp.start()
        sends.append(cp)
    cp = text_core(3, place)
    cp.start()
    sends.append(cp)
    for k in (0, 2, 1):
        for p in range(PARTS):
            ring_wait(p, 1, k)
            last_send(p, k + 1)
    for p in range(PARTS):
        core_send(p, 0)

    def column_peer(k):
        n = (place + k + 1) % NC
        return n, (n // 2 * 4 + xh * 2 + n % 2, d)

    def column_copy(src, dst, k, to, ssem, rsem):
        return pltpu.make_async_remote_copy(
            src_ref=src, dst_ref=dst, send_sem=ssem.at[k], recv_sem=rsem.at[k], device_id=to, device_id_type=MESH
        )

    def column_wait(buf, k, ssem, rsem):
        frm, dev = column_peer(NC - 2 - k)
        column_copy(buf.at[frm], buf.at[frm], k, dev, ssem, rsem).wait_recv()

    for k in range(NC - 1):
        n, to = column_peer(k)
        cp = column_copy(asrc.at[n], arcv.at[place], k, to, a_send, a_recv)
        cp.start()
        sends.append(cp)
    first = pl.multiple_of((z * 4 + core) * 128, 128)
    rows_of = [wv[pl.ds(pl.multiple_of(first + 256 * h, 128), 128), :] for h in range(2)]
    wh[...] = mm(jnp.concatenate(rows_of, axis=0), headv[...])

    for k in (0, 2, 1):
        frm = step_of("z", -1 - k)
        idx = frm["z"] * 2 + core
        text_copy(k, idx, frm).wait_recv()
        cp = text_core(k, idx)
        cp.start()
        sends.append(cp)
    for k in (0, 2, 1):
        for p in range(PARTS):
            last_wait(p, k)
            core_send(p, k + 1)
    for p in range(PARTS):
        for q in range(4):
            core_copy(p, q, False).wait_recv()

    scale = jnp.exp(jnp.full((1, 128), lp_ref[0], f32))[:, 0:1]
    bias = jnp.full((1, 128), lp_ref[1], f32)[:, 0:1]

    def pair(dots, gid, ids):
        val = scale * dots + bias
        same = gid == ids
        arg = jnp.where(same, -val, val)
        coef = jnp.where(same, -scale, scale) * pl.reciprocal(1.0 + jnp.exp(-arg), approx=True)
        return arg, coef

    def row_copy(src, dst, k, ssem, rsem):
        n = (seat + k + 1) % NR
        return pltpu.make_async_remote_copy(
            src_ref=src, dst_ref=dst, send_sem=ssem.at[k], recv_sem=rsem.at[k],
            device_id=(z * 4 + n // ND * 2 + core, n % ND), device_id_type=MESH,
        )

    def row_wait(buf, k, ssem, rsem):
        frm = (seat + NR - 1 - k) % NR
        row_copy(buf.at[frm], buf.at[frm], k, ssem, rsem).wait_recv()

    for k in (0, 2, 1):
        text_core(k, step_of("z", -1 - k)["z"] * 2 + 1 - core).wait_recv()
    text_core(3, place + 1 - 2 * core).wait_recv()

    owner = tbuf[:, :, E:PW].reshape(SLOTS, 128).astype(f32)[:, 0:1]
    row = iota((SLOTS, 1), 0) // CAPS
    block = ((row // 2 * 4 + row % 2 + xh * 2) * 128).astype(f32)
    gid = jnp.where(owner >= 0.0, owner + block, -1.0)
    texts = tbuf[:, :, 0:E].reshape(SLOTS, E)
    group = img[z, :, core].reshape(GR, E)
    lane_g = iota((1, GR), 1)
    ids_g = ((z * 4 + core) * 128 + lane_g + lane_g // 128 * 128).astype(f32)
    arg, coef = pair(mm_nt(texts, group), gid, ids_g)
    dimg_part = mm(coef.T.astype(bf16), texts)
    c3as[...] = dimg_part.reshape(NR, 16, E).astype(bf16)
    c3ar[seat] = c3as[seat]
    for k in range(NR - 1):
        cp = row_copy(c3as.at[(seat + k + 1) % NR], c3ar.at[seat], k, ca_send, ca_recv)
        cp.start()
        sends.append(cp)
    soft = jnp.maximum(arg, 0.0) + jnp.log1p(jnp.exp(-jnp.abs(arg)))
    loss_part = jnp.sum(jnp.where(gid >= 0.0, soft, 0.0), axis=0, keepdims=True)

    for k in range(NC - 1):
        column_wait(arcv, k, a_send, a_recv)
    share = jnp.concatenate([arcv[:, h].reshape(SLOTS, 128) for h in range(2)], axis=1).astype(f32)
    share_t = share.T.astype(bf16)
    bacc[...] = jnp.zeros((GR + CAPS, E), f32)
    rsacc[...] = jnp.zeros((SLOTS, 1), f32)

    def pair_chunk(c, _):
        chunk = img[c].reshape(512, E)
        dots = mm_nt(tbuf[:, :, 0:E].reshape(SLOTS, E), chunk)
        _, coef = pair(dots, gid, (iota((1, 512), 1) + c * 512).astype(f32))
        rsacc[...] += jnp.sum(coef * dots, axis=1, keepdims=True)
        coefs[...] = coef.astype(bf16)
        zc[0:GR, :] = mm(share_t, coefs[...]).astype(bf16)
        zc[GR : GR + CAPS, :] = coefs[pl.ds(pl.multiple_of(place * CAPS, CAPS), CAPS), :]
        bacc[...] += mm(zc[...], chunk)
        return 0

    lax.fori_loop(0, 4, pair_chunk, 0, unroll=UNROLL)

    minus_t = (share * rsacc[...]).T.astype(bf16)
    bpart = bacc[0:GR, :] - mm(minus_t, texts)
    c3bs[...] = bpart.reshape(NR, 16, E).astype(bf16)
    c3br[seat] = c3bs[seat]
    gain_part = jnp.broadcast_to(jnp.sum(bpart * wh[...], axis=1, keepdims=True), (GR, 128)).T[0:1]
    gbuf[seat] = jnp.zeros((8, 128), f32)
    for h in range(2):
        gbuf[seat, h : h + 1, :] = loss_part[:, 128 * h : 128 * h + 128]
        gbuf[seat, 2 + h : 3 + h, :] = gain_part[:, 128 * h : 128 * h + 128]
    for k in range(NR - 1):
        cp = row_copy(gbuf.at[seat], gbuf.at[seat], k, g_send, g_recv)
        cp.start()
        sends.append(cp)
    for k in range(NR - 1):
        cp = row_copy(c3bs.at[(seat + k + 1) % NR], c3br.at[seat], k, cb_send, cb_recv)
        cp.start()
        sends.append(cp)

    dtext = bacc[GR : GR + CAPS, :]
    dproj = (
        scale_inv * (dtext - text_unit * jnp.sum(text_unit * dtext, axis=1, keepdims=True))
    ).astype(bf16)
    live = jnp.where(own_col >= 0.0, rcount, 0.0)

    def dcap_tile(i, _):
        rows = pl.ds(pl.multiple_of(i * TN, TN), TN)
        dpool = mm_nt(dproj, headv[rows, :]).astype(bf16).astype(f32)
        dc = (dpool * live).astype(bf16)
        dcap[:, rows] = dc
        stack[0:CAPS, rows] = dc
        return 0

    lax.fori_loop(0, DT // TN, dcap_tile, 0)

    for k in range(NR - 1):
        row_wait(gbuf, k, g_send, g_recv)
    gsum = jnp.sum(gbuf[...], axis=0)
    g2[place] = gsum
    for k in range(NC - 1):
        _, to = column_peer(k)
        cp = column_copy(g2.at[place], g2.at[place], k, to, h_send, h_recv)
        cp.start()
        sends.append(cp)

    def dnorm_tile(i, _):
        rows = pl.ds(pl.multiple_of(i * TN, TN), TN)
        hi, lo = split2(mm_nt(dcap[...], wv[rows, :]) * gain_ref[:, rows])
        stack[CAPS : 2 * CAPS, rows] = hi
        stack[2 * CAPS : 3 * CAPS, rows] = hi
        stack[3 * CAPS : 4 * CAPS, rows] = lo
        return 0

    lax.fori_loop(0, DT // TN, dnorm_tile, 0)

    stores = []
    for i in range(4):
        rows = pl.ds(i * 128, 128)
        xb = tok[rows, :]
        lc = lcol[rows, :]
        q = mm_nt(xb, stack[...])
        mine = (segt[rows, :] == cap_of) & ((kind == 1) | (kind == 3))
        mean = jnp.sum(jnp.where(mine, q, 0.0), axis=1, keepdims=True) * (1.0 / DT)
        inv = invc[rows, :]
        drop = inv * inv * inv * mean
        full = mm(lc.astype(bf16), stack[...])
        stage[rows, :] = (full - xb.astype(f32) * drop).astype(bf16)
        cp = pltpu.make_async_copy(stage.at[rows, :], dtok_hbm.at[rows, :], st_sem.at[i])
        cp.start()
        stores.append(cp)

    for k in range(NR - 1):
        row_wait(c3ar, k, ca_send, ca_recv)
    dimg = jnp.sum(c3ar[...].astype(f32), axis=0)
    dimg_out[...] = img_inv * (dimg - img_unit * jnp.sum(img_unit * dimg, axis=1, keepdims=True))
    for k in range(NR - 1):
        row_wait(c3br, k, cb_send, cb_recv)
    mine = iota((16, 128), 1) == iota((16, 128), 0) + 16 * d

    def own_rows(row):
        return jnp.sum(jnp.where(mine, jnp.broadcast_to(row, (16, 128)), 0.0), axis=1, keepdims=True)

    gain_col = own_rows(gain_ref[:, pl.ds(pl.multiple_of(b * 128, 128), 128)])
    hi, lo = split2(jnp.sum(c3br[...].astype(f32), axis=0) * gain_col)
    both = jnp.concatenate([hi, lo], axis=0)

    def dw_tile(i, _):
        rows = pl.ds(pl.multiple_of(i * TN, TN), TN)
        dw = mm_nt(both, headv[rows, :])
        dw_out[:, rows] = dw[0:16] + dw[16:32]
        return 0

    lax.fori_loop(0, DT // TN, dw_tile, 0)

    col = own_rows(jnp.where(xh == 0, gsum[0:1], gsum[1:2]) * (1.0 / TOTAL))
    loss_out[...] = jnp.sum(jnp.where(iota((16, 16), 0) == iota((16, 16), 1), col, 0.0), axis=0, keepdims=True)

    for k in range(NC - 1):
        column_wait(g2, k, h_send, h_recv)
    for r in range(NB):
        h = r // 2 % 2
        dgain_out[r : r + 1, :] = g2[r // 4 * 2 + r % 2, 2 + h : 3 + h, :]

    for cp in stores:
        cp.wait()
    for cp in sends:
        cp.wait_send()


def hand_over(loss, dtok, dw, dgain, dimg, loss_out, dtok_out, dw_out, dgain_out, dimg_out, buf, ins, outs):
    reads = []
    for i in range(4):
        cp = pltpu.make_async_copy(dtok.at[pl.ds(i * 128, 128), :], buf.at[pl.ds(i * 128, 128), :], ins.at[i])
        cp.start()
        reads.append(cp)
    loss_out[...] = loss[...]
    dw_out[...] = dw[...]
    dgain_out[...] = dgain[...]
    dimg_out[...] = dimg[...]
    writes = []
    for i in range(4):
        reads[i].wait()
        cp = pltpu.make_async_copy(buf.at[pl.ds(i * 128, 128), :], dtok_out.at[pl.ds(i * 128, 128), :], outs.at[i])
        cp.start()
        writes.append(cp)
    for cp in writes:
        cp.wait()


def per_device(tokens, segment_ids, owners, images, weight, gain, head, logit_params):
    vmem = pl.BlockSpec(memory_space=pltpu.VMEM)
    hbm = pl.BlockSpec(memory_space=pl.ANY)
    dma = pltpu.SemaphoreType.DMA
    shapes = (
        jax.ShapeDtypeStruct((1, 16), f32),
        jax.ShapeDtypeStruct((ROWS, DT), bf16),
        jax.ShapeDtypeStruct((16, DT), f32),
        jax.ShapeDtypeStruct((16, 128), f32),
        jax.ShapeDtypeStruct((16, E), f32),
    )
    held = pl.pallas_call(
        kernel,
        out_shape=shapes,
        in_specs=[hbm, hbm, hbm, hbm, hbm, hbm, hbm, pl.BlockSpec(memory_space=pltpu.SMEM)],
        out_specs=(vmem, hbm, vmem, vmem, vmem),
        scratch_shapes=[
            pltpu.VMEM((ROWS, DT), bf16),
            pltpu.VMEM((DT, DT), bf16),
            pltpu.VMEM((DT, E), bf16),
            pltpu.VMEM((4, 2, 2, 4, 2, 16, E), bf16),
            pltpu.VMEM((ROWS, 128), f32),
            pltpu.VMEM((ROWS, 128), f32),
            pltpu.VMEM((ROWS, 1), f32),
            pltpu.VMEM((CAPS, DT), f32),
            pltpu.VMEM((CAPS, DT), f32),
            pltpu.VMEM((2 * CAPS, DT), bf16),
            pltpu.VMEM((CAPS, DT), bf16),
            pltpu.VMEM((NC, 2, CAPS, 128), bf16),
            pltpu.VMEM((NC, 2, CAPS, 128), bf16),
            pltpu.VMEM((NC, CAPS, PW), bf16),
            pltpu.VMEM((CAPS, DT), bf16),
            pltpu.VMEM((4 * CAPS, DT), bf16),
            pltpu.VMEM((1, ROWS), jnp.int32),
            pltpu.VMEM((1, CAPS), jnp.int32),
            pltpu.VMEM((16, E), bf16),
            pltpu.VMEM((1, DT), f32),
            pltpu.VMEM((ROWS, DT), bf16),
            pltpu.VMEM((GR, E), f32),
            pltpu.VMEM((SLOTS, 512), bf16),
            pltpu.VMEM((GR + CAPS, 512), bf16),
            pltpu.VMEM((GR + CAPS, E), f32),
            pltpu.VMEM((SLOTS, 1), f32),
            pltpu.VMEM((NR, 16, E), bf16),
            pltpu.VMEM((NR, 16, E), bf16),
            pltpu.VMEM((NR, 16, E), bf16),
            pltpu.VMEM((NR, 16, E), bf16),
            pltpu.VMEM((NR, 8, 128), f32),
            pltpu.VMEM((NC, 8, 128), f32),
            dma((5,)),
            dma((DT // TN,)),
            dma((4,)),
            dma((4,)),
            dma((PARTS, 2, 3)),
            dma((PARTS, 2, 3)),
            dma((PARTS, 4, 3)),
            dma((PARTS, 4, 3)),
            dma((PARTS, 4)),
            dma((PARTS, 4)),
            dma((3,)),
            dma((3,)),
            dma((4,)),
            dma((4,)),
            dma((NC - 1,)),
            dma((NC - 1,)),
            dma((NR - 1,)),
            dma((NR - 1,)),
            dma((NR - 1,)),
            dma((NR - 1,)),
            dma((NR - 1,)),
            dma((NR - 1,)),
            dma((NC - 1,)),
            dma((NC - 1,)),
        ],
        compiler_params=pltpu.CompilerParams(
            collective_id=0, has_side_effects=True, vmem_limit_bytes=56 * 1024 * 1024
        ),
    )(tokens, weight, head, segment_ids, owners, images, gain.reshape(1, DT), logit_params)
    loss, d_tokens, d_weight, d_gain, d_images = pl.pallas_call(
        hand_over,
        out_shape=shapes,
        in_specs=[vmem, hbm, vmem, vmem, vmem],
        out_specs=(vmem, hbm, vmem, vmem, vmem),
        scratch_shapes=[pltpu.VMEM((ROWS, DT), bf16), dma((4,)), dma((4,))],
        compiler_params=pltpu.CompilerParams(vmem_limit_bytes=56 * 1024 * 1024),
    )(*held)
    return loss.reshape(16), d_tokens, d_weight, d_gain.reshape(DT), d_images


def solution(mesh):
    rows = P(("blk", "dp"), None)
    return jax.shard_map(
        per_device,
        mesh=mesh,
        in_specs=(rows, rows, rows, rows, P(), P(), P(), P()),
        out_specs=(P(("blk", "dp")), rows, rows, P(), rows),
        check_vma=False,
    )
```

```python
import functools

import jax
import jax.numpy as jnp
from jax import lax
from jax.experimental import pallas as pl
from jax.experimental.pallas import tpu as pltpu
from jax.sharding import PartitionSpec as P

f32 = jnp.float32
bf16 = jnp.bfloat16
MESH = pl.DeviceIdType.MESH

DT = 2048
E = 1152
ROWS = 512
CAPS = 32
NB = 16
ND = 8
TOTAL = 2048
NC = 8
NR = 16
SLOTS = NC * CAPS
GR = NR * 16
PW = E + 128
PARTS = 3
ORDERS = (("x", "y", "z"), ("y", "z", "x"), ("z", "x", "y"))
COLUMNS = ((0, 128), (128, 384), (512, 640))
TN = 512
UNROLL = True


def mm(a, b):
    return lax.dot_general(a, b, (((1,), (0,)), ((), ())), preferred_element_type=f32)


def mm_nt(a, b):
    return lax.dot_general(a, b, (((1,), (1,)), ((), ())), preferred_element_type=f32)


def split2(v):
    hi = v.astype(bf16)
    return hi, (v - hi.astype(f32)).astype(bf16)


def iota(shape, dim):
    return lax.broadcasted_iota(jnp.int32, shape, dim)


def kernel(
    tok_hbm, w_hbm, head_hbm, seg_hbm, own_hbm, img_hbm, gain_hbm, lp_ref,
    loss_out, dtok_hbm, dw_out, dgain_out, dimg_out,
    tok, wv, headv, img, lcol, segt, invc, xs, xp, npst, pooled, asrc, arcv, tbuf, dcap, stack,
    seg_ref, own_ref, img_ref, gain_ref, stage, wh, coefs, zc, bacc, rsacc, c3as, c3ar, c3bs, c3br, gbuf, g2,
    ld_sem, w_sem, in_sem, st_sem,
    i_send, i_recv, j_send, j_recv, ic_send, ic_recv, t_send, t_recv, tc_send, tc_recv, a_send, a_recv,
    ca_send, ca_recv, cb_send, cb_recv, g_send, g_recv, h_send, h_recv,
):
    b = lax.axis_index("blk")
    d = lax.axis_index("dp")
    z, xh, core = b // 4, (b // 2) % 2, b % 2
    y, xl = d // 2, d % 2
    x = xh * 2 + xl
    sib = (b + 1 - 2 * core, d)
    place = z * 2 + core
    seat = xh * ND + d

    here = {"x": x, "y": y, "z": z, "core": core}

    def device(at):
        return (at["z"] * 4 + (at["x"] // 2) * 2 + at["core"], at["y"] * 2 + at["x"] % 2)

    def step_of(axis, n):
        at = dict(here)
        at[axis] = (here[axis] + 4 + n) % 4
        return at

    barrier = pltpu.get_barrier_semaphore()
    pl.semaphore_signal(barrier, inc=1, device_id=sib, device_id_type=MESH)
    for axis in ("x", "y", "z"):
        for k in (1, 3, 2):
            pl.semaphore_signal(barrier, inc=1, device_id=device(step_of(axis, k)), device_id_type=MESH)

    inputs = []
    for i, (src, dst) in enumerate(((img_hbm, img_ref), (seg_hbm, seg_ref), (own_hbm, own_ref), (gain_hbm, gain_ref))):
        cp = pltpu.make_async_copy(src, dst, in_sem.at[i])
        cp.start()
        inputs.append(cp)
    loads = []
    for i in range(4):
        cp = pltpu.make_async_copy(
            tok_hbm.at[pl.ds(i * 128, 128), :], tok.at[pl.ds(i * 128, 128), :], ld_sem.at[i]
        )
        cp.start()
        loads.append(cp)
    wloads = []
    for i in range(DT // TN):
        cp = pltpu.make_async_copy(
            w_hbm.at[:, pl.ds(i * TN, TN)], wv.at[:, pl.ds(i * TN, TN)], w_sem.at[i]
        )
        cp.start()
        wloads.append(cp)
    hload = pltpu.make_async_copy(head_hbm, headv, ld_sem.at[4])
    hload.start()

    inputs[0].wait()
    im = img_ref[...].astype(f32)
    img_inv = lax.rsqrt(jnp.sum(im * im, axis=1, keepdims=True) + 1e-06)
    img_unit = im * img_inv
    img[z, xh, core, y, xl] = img_unit.astype(bf16)

    sends = []

    def region(p, at):
        def pick(name):
            return slice(None) if at[name] is None else at[name]

        xx = at["x"]
        return img.at[
            pick("z"),
            slice(None) if xx is None else xx // 2,
            at["core"],
            pick("y"),
            slice(None) if xx is None else xx % 2,
            :,
            pl.ds(*COLUMNS[p]),
        ]

    def ring_region(p, done, where):
        at = dict(where)
        for name in done:
            at[name] = None
        return region(p, at)

    def ring_copy(p, s, k, where, to):
        ref = ring_region(p, ORDERS[p][:s], where)
        return pltpu.make_async_remote_copy(
            src_ref=ref, dst_ref=ref, send_sem=i_send.at[p, s, k], recv_sem=i_recv.at[p, s, k],
            device_id=device(to), device_id_type=MESH,
        )

    def last_copy(p, j, k, where, to):
        first, second, _ = ORDERS[p]
        at = dict(where)
        at[second] = (here[second] + 4 - j) % 4
        ref = ring_region(p, (first,), at)
        return pltpu.make_async_remote_copy(
            src_ref=ref, dst_ref=ref, send_sem=j_send.at[p, j, k], recv_sem=j_recv.at[p, j, k],
            device_id=device(to), device_id_type=MESH,
        )

    def ring_send(p, s):
        for k in range(3):
            cp = ring_copy(p, s, k, here, step_of(ORDERS[p][s], k + 1))
            cp.start()
            sends.append(cp)

    def ring_wait(p, s, k):
        frm = step_of(ORDERS[p][s], -1 - k)
        ring_copy(p, s, k, frm, frm).wait_recv()

    def last_send(p, j):
        for k in range(3):
            cp = last_copy(p, j, k, here, step_of(ORDERS[p][2], k + 1))
            cp.start()
            sends.append(cp)

    def last_wait(p, k):
        frm = step_of(ORDERS[p][2], -1 - k)
        for j in range(4):
            last_copy(p, j, k, frm, frm).wait_recv()

    def core_copy(p, q, own):
        order = ORDERS[p]
        at = dict(here)
        for name in order[:2]:
            at[name] = None
        if q:
            at[order[2]] = (here[order[2]] + 4 - q) % 4
        if not own:
            at["core"] = 1 - core
        ref = region(p, at)
        return pltpu.make_async_remote_copy(
            src_ref=ref, dst_ref=ref, send_sem=ic_send.at[p, q], recv_sem=ic_recv.at[p, q],
            device_id=sib, device_id_type=MESH,
        )

    def core_send(p, q):
        cp = core_copy(p, q, True)
        cp.start()
        sends.append(cp)

    pl.semaphore_wait(barrier, 10)
    for p in range(PARTS):
        ring_send(p, 0)

    for cp in inputs[1:]:
        cp.wait()
    segf = seg_ref[...].astype(f32)
    segt[...] = jnp.broadcast_to(segf, (128, ROWS)).T
    lane = iota((128, 128), 1)
    cap_of = (lane % CAPS).astype(f32)
    kind = lane // CAPS

    def token_rows(i):
        loads[i].wait()
        rows = pl.ds(i * 128, 128)
        xx = tok[rows, :].astype(f32)
        inv = lax.rsqrt(jnp.sum(xx * xx, axis=1, keepdims=True) * (1.0 / DT) + 1e-06)
        invc[rows, :] = inv
        hi = inv.astype(bf16).astype(f32)
        lo = inv - hi
        val = jnp.where(kind == 0, 1.0, jnp.where(kind == 2, lo, hi))
        lcol[rows, :] = jnp.where(segt[rows, :] == cap_of, val, 0.0)

    for i in range(4):
        token_rows(i)

    lrow = lcol[...].T.astype(bf16)

    def pool_tile(i, _):
        cols = pl.ds(pl.multiple_of(i * TN, TN), TN)
        acc = mm(lrow, tok[:, cols])
        xs[:, cols] = acc[0:CAPS]
        xpt = acc[CAPS : 2 * CAPS] + acc[2 * CAPS : 3 * CAPS]
        xp[:, cols] = xpt
        hi, lo = split2(xpt * gain_ref[:, cols])
        npst[0:CAPS, cols] = hi
        npst[CAPS : 2 * CAPS, cols] = lo
        return 0

    lax.fori_loop(0, DT // TN, pool_tile, 0)

    sel = (jnp.broadcast_to(segf, (CAPS, ROWS)) == iota((CAPS, ROWS), 0).astype(f32)).astype(f32)
    rcount = 1.0 / jnp.maximum(jnp.sum(sel, axis=1, keepdims=True), 1.0)
    ownf = own_ref[...].astype(f32)
    own_col = jnp.sum(
        jnp.where(iota((CAPS, CAPS), 0) == iota((CAPS, CAPS), 1), jnp.broadcast_to(ownf, (CAPS, CAPS)), 0.0),
        axis=1,
        keepdims=True,
    )

    for i in range(DT // TN):
        if i == 2:
            for p in (2, 1, 0):
                for k in range(3):
                    ring_wait(p, 0, k)
                ring_send(p, 1)
            for p in (2, 1, 0):
                last_send(p, 0)
        wloads[i].wait()
        cols = pl.ds(i * TN, TN)
        yy = mm(npst[...], wv[:, cols])
        pooled[:, cols] = ((xs[:, cols] + yy[0:CAPS] + yy[CAPS : 2 * CAPS]) * rcount).astype(bf16)

    hload.wait()
    proj = mm(pooled[...], headv[...])
    scale_inv = lax.rsqrt(jnp.sum(proj * proj, axis=1, keepdims=True) + 1e-06)
    text_unit = proj * scale_inv
    text = text_unit.astype(bf16)
    tbuf[place, :, 0:E] = text
    tbuf[place, :, E:PW] = jnp.broadcast_to(own_col, (CAPS, 128)).astype(bf16)
    factor = scale_inv * rcount
    for j in range(NB):
        cols = pl.ds(j * 128, 128)
        asrc[j // 4 * 2 + j % 2, j // 2 % 2] = (xp[:, cols] * factor).astype(bf16)
    arcv[place] = asrc[place]

    def text_copy(k, idx, to):
        return pltpu.make_async_remote_copy(
            src_ref=tbuf.at[idx], dst_ref=tbuf.at[idx], send_sem=t_send.at[k], recv_sem=t_recv.at[k],
            device_id=device(to), device_id_type=MESH,
        )

    def text_core(k, idx):
        return pltpu.make_async_remote_copy(
            src_ref=tbuf.at[idx], dst_ref=tbuf.at[idx], send_sem=tc_send.at[k], recv_sem=tc_recv.at[k],
            device_id=sib, device_id_type=MESH,
        )

    for k in range(3):
        cp = text_copy(k, place, step_of("z", k + 1))
        cp.start()
        sends.append(cp)
    cp = text_core(3, place)
    cp.start()
    sends.append(cp)
    for p in (2, 1, 0):
        for k in (0, 2, 1):
            ring_wait(p, 1, k)
            last_send(p, k + 1)
    for p in range(PARTS):
        core_send(p, 0)

    def column_peer(k):
        n = (place + k + 1) % NC
        return n, (n // 2 * 4 + xh * 2 + n % 2, d)

    def column_copy(src, dst, k, to, ssem, rsem):
        return pltpu.make_async_remote_copy(
            src_ref=src, dst_ref=dst, send_sem=ssem.at[k], recv_sem=rsem.at[k], device_id=to, device_id_type=MESH
        )

    def column_wait(buf, k, ssem, rsem):
        frm, dev = column_peer(NC - 2 - k)
        column_copy(buf.at[frm], buf.at[frm], k, dev, ssem, rsem).wait_recv()

    for k in range(NC - 1):
        n, to = column_peer(k)
        cp = column_copy(asrc.at[n], arcv.at[place], k, to, a_send, a_recv)
        cp.start()
        sends.append(cp)
    first = pl.multiple_of((z * 4 + core) * 128, 128)
    rows_of = [wv[pl.ds(pl.multiple_of(first + 256 * h, 128), 128), :] for h in range(2)]
    wh[...] = mm(jnp.concatenate(rows_of, axis=0), headv[...])

    for k in (0, 2, 1):
        frm = step_of("z", -1 - k)
        idx = frm["z"] * 2 + core
        text_copy(k, idx, frm).wait_recv()
        cp = text_core(k, idx)
        cp.start()
        sends.append(cp)
    for p in range(PARTS):
        for k in (0, 2, 1):
            last_wait(p, k)
            core_send(p, k + 1)
    for p in range(PARTS):
        for q in range(4):
            core_copy(p, q, False).wait_recv()

    scale = jnp.exp(jnp.full((1, 128), lp_ref[0], f32))[:, 0:1]
    bias = jnp.full((1, 128), lp_ref[1], f32)[:, 0:1]

    def pair(dots, gid, ids):
        val = scale * dots + bias
        same = gid == ids
        arg = jnp.where(same, -val, val)
        coef = jnp.where(same, -scale, scale) * pl.reciprocal(1.0 + jnp.exp(-arg), approx=True)
        return arg, coef

    def row_copy(src, dst, k, ssem, rsem):
        n = (seat + k + 1) % NR
        return pltpu.make_async_remote_copy(
            src_ref=src, dst_ref=dst, send_sem=ssem.at[k], recv_sem=rsem.at[k],
            device_id=(z * 4 + n // ND * 2 + core, n % ND), device_id_type=MESH,
        )

    def row_wait(buf, k, ssem, rsem):
        frm = (seat + NR - 1 - k) % NR
        row_copy(buf.at[frm], buf.at[frm], k, ssem, rsem).wait_recv()

    for k in (0, 2, 1):
        text_core(k, step_of("z", -1 - k)["z"] * 2 + 1 - core).wait_recv()
    text_core(3, place + 1 - 2 * core).wait_recv()

    owner = tbuf[:, :, E:PW].reshape(SLOTS, 128).astype(f32)[:, 0:1]
    row = iota((SLOTS, 1), 0) // CAPS
    block = ((row // 2 * 4 + row % 2 + xh * 2) * 128).astype(f32)
    gid = jnp.where(owner >= 0.0, owner + block, -1.0)
    texts = tbuf[:, :, 0:E].reshape(SLOTS, E)
    group = img[z, :, core].reshape(GR, E)
    lane_g = iota((1, GR), 1)
    ids_g = ((z * 4 + core) * 128 + lane_g + lane_g // 128 * 128).astype(f32)
    arg, coef = pair(mm_nt(texts, group), gid, ids_g)
    dimg_part = mm(coef.T.astype(bf16), texts)
    c3as[...] = dimg_part.reshape(NR, 16, E).astype(bf16)
    c3ar[seat] = c3as[seat]
    for k in range(NR - 1):
        cp = row_copy(c3as.at[(seat + k + 1) % NR], c3ar.at[seat], k, ca_send, ca_recv)
        cp.start()
        sends.append(cp)
    soft = jnp.maximum(arg, 0.0) + jnp.log1p(jnp.exp(-jnp.abs(arg)))
    loss_part = jnp.sum(jnp.where(gid >= 0.0, soft, 0.0), axis=0, keepdims=True)

    for k in range(NC - 1):
        column_wait(arcv, k, a_send, a_recv)
    share = jnp.concatenate([arcv[:, h].reshape(SLOTS, 128) for h in range(2)], axis=1).astype(f32)
    share_t = share.T.astype(bf16)
    bacc[...] = jnp.zeros((GR + CAPS, E), f32)
    rsacc[...] = jnp.zeros((SLOTS, 1), f32)

    def pair_chunk(c, _):
        chunk = img[c].reshape(512, E)
        dots = mm_nt(tbuf[:, :, 0:E].reshape(SLOTS, E), chunk)
        _, coef = pair(dots, gid, (iota((1, 512), 1) + c * 512).astype(f32))
        rsacc[...] += jnp.sum(coef * dots, axis=1, keepdims=True)
        coefs[...] = coef.astype(bf16)
        zc[0:GR, :] = mm(share_t, coefs[...]).astype(bf16)
        zc[GR : GR + CAPS, :] = coefs[pl.ds(pl.multiple_of(place * CAPS, CAPS), CAPS), :]
        bacc[...] += mm(zc[...], chunk)
        return 0

    lax.fori_loop(0, 4, pair_chunk, 0, unroll=UNROLL)

    minus_t = (share * rsacc[...]).T.astype(bf16)
    bpart = bacc[0:GR, :] - mm(minus_t, texts)
    c3bs[...] = bpart.reshape(NR, 16, E).astype(bf16)
    c3br[seat] = c3bs[seat]
    gain_part = jnp.broadcast_to(jnp.sum(bpart * wh[...], axis=1, keepdims=True), (GR, 128)).T[0:1]
    gbuf[seat] = jnp.zeros((8, 128), f32)
    for h in range(2):
        gbuf[seat, h : h + 1, :] = loss_part[:, 128 * h : 128 * h + 128]
        gbuf[seat, 2 + h : 3 + h, :] = gain_part[:, 128 * h : 128 * h + 128]
    for k in range(NR - 1):
        cp = row_copy(gbuf.at[seat], gbuf.at[seat], k, g_send, g_recv)
        cp.start()
        sends.append(cp)
    for k in range(NR - 1):
        cp = row_copy(c3bs.at[(seat + k + 1) % NR], c3br.at[seat], k, cb_send, cb_recv)
        cp.start()
        sends.append(cp)

    dtext = bacc[GR : GR + CAPS, :]
    dproj = (
        scale_inv * (dtext - text_unit * jnp.sum(text_unit * dtext, axis=1, keepdims=True))
    ).astype(bf16)
    live = jnp.where(own_col >= 0.0, rcount, 0.0)

    def dcap_tile(i, _):
        rows = pl.ds(pl.multiple_of(i * TN, TN), TN)
        dpool = mm_nt(dproj, headv[rows, :]).astype(bf16).astype(f32)
        dc = (dpool * live).astype(bf16)
        dcap[:, rows] = dc
        stack[0:CAPS, rows] = dc
        return 0

    lax.fori_loop(0, DT // TN, dcap_tile, 0)

    for k in range(NR - 1):
        row_wait(gbuf, k, g_send, g_recv)
    gsum = jnp.sum(gbuf[...], axis=0)
    g2[place] = gsum
    for k in range(NC - 1):
        _, to = column_peer(k)
        cp = column_copy(g2.at[place], g2.at[place], k, to, h_send, h_recv)
        cp.start()
        sends.append(cp)

    def dnorm_tile(i, _):
        rows = pl.ds(pl.multiple_of(i * TN, TN), TN)
        hi, lo = split2(mm_nt(dcap[...], wv[rows, :]) * gain_ref[:, rows])
        stack[CAPS : 2 * CAPS, rows] = hi
        stack[2 * CAPS : 3 * CAPS, rows] = hi
        stack[3 * CAPS : 4 * CAPS, rows] = lo
        return 0

    lax.fori_loop(0, DT // TN, dnorm_tile, 0)

    stores = []
    for i in range(4):
        rows = pl.ds(i * 128, 128)
        xb = tok[rows, :]
        lc = lcol[rows, :]
        q = mm_nt(xb, stack[...])
        mine = (segt[rows, :] == cap_of) & ((kind == 1) | (kind == 3))
        mean = jnp.sum(jnp.where(mine, q, 0.0), axis=1, keepdims=True) * (1.0 / DT)
        inv = invc[rows, :]
        drop = inv * inv * inv * mean
        full = mm(lc.astype(bf16), stack[...])
        stage[rows, :] = (full - xb.astype(f32) * drop).astype(bf16)
        cp = pltpu.make_async_copy(stage.at[rows, :], dtok_hbm.at[rows, :], st_sem.at[i])
        cp.start()
        stores.append(cp)

    for k in range(NR - 1):
        row_wait(c3ar, k, ca_send, ca_recv)
    dimg = jnp.sum(c3ar[...].astype(f32), axis=0)
    dimg_out[...] = img_inv * (dimg - img_unit * jnp.sum(img_unit * dimg, axis=1, keepdims=True))
    for k in range(NR - 1):
        row_wait(c3br, k, cb_send, cb_recv)
    mine = iota((16, 128), 1) == iota((16, 128), 0) + 16 * d

    def own_rows(row):
        return jnp.sum(jnp.where(mine, jnp.broadcast_to(row, (16, 128)), 0.0), axis=1, keepdims=True)

    gain_col = own_rows(gain_ref[:, pl.ds(pl.multiple_of(b * 128, 128), 128)])
    hi, lo = split2(jnp.sum(c3br[...].astype(f32), axis=0) * gain_col)
    both = jnp.concatenate([hi, lo], axis=0)

    def dw_tile(i, _):
        rows = pl.ds(pl.multiple_of(i * TN, TN), TN)
        dw = mm_nt(both, headv[rows, :])
        dw_out[:, rows] = dw[0:16] + dw[16:32]
        return 0

    lax.fori_loop(0, DT // TN, dw_tile, 0)

    col = own_rows(jnp.where(xh == 0, gsum[0:1], gsum[1:2]) * (1.0 / TOTAL))
    loss_out[...] = jnp.sum(jnp.where(iota((16, 16), 0) == iota((16, 16), 1), col, 0.0), axis=0, keepdims=True)

    for k in range(NC - 1):
        column_wait(g2, k, h_send, h_recv)
    for r in range(NB):
        h = r // 2 % 2
        dgain_out[r : r + 1, :] = g2[r // 4 * 2 + r % 2, 2 + h : 3 + h, :]

    for cp in stores:
        cp.wait()
    for cp in sends:
        cp.wait_send()


def hand_over(
    loss, dtok, dw, dgain, dimg, loss_out, dtok_out, dw_out, dgain_out, dimg_out,
    loss_buf, dtok_buf, dw_buf, dgain_buf, dimg_buf, ins, outs,
):
    trips = [
        (dtok.at[rows, :], dtok_buf.at[rows, :], dtok_out.at[rows, :])
        for rows in [pl.ds(i * 64, 64) for i in range(8)]
    ]
    trips += [
        (dw, dw_buf, dw_out), (dimg, dimg_buf, dimg_out), (dgain, dgain_buf, dgain_out), (loss, loss_buf, loss_out)
    ]
    reads, writes = [], []
    for i, (src, buf, _) in enumerate(trips):
        cp = pltpu.make_async_copy(src, buf, ins.at[i])
        cp.start()
        reads.append(cp)
    for i, (_, buf, dst) in enumerate(trips):
        reads[i].wait()
        cp = pltpu.make_async_copy(buf, dst, outs.at[i])
        cp.start()
        writes.append(cp)
    for cp in writes:
        cp.wait()


def per_device(tokens, segment_ids, owners, images, weight, gain, head, logit_params):
    vmem = pl.BlockSpec(memory_space=pltpu.VMEM)
    hbm = pl.BlockSpec(memory_space=pl.ANY)
    dma = pltpu.SemaphoreType.DMA
    shapes = (
        jax.ShapeDtypeStruct((1, 16), f32),
        jax.ShapeDtypeStruct((ROWS, DT), bf16),
        jax.ShapeDtypeStruct((16, DT), f32),
        jax.ShapeDtypeStruct((16, 128), f32),
        jax.ShapeDtypeStruct((16, E), f32),
    )
    held = pl.pallas_call(
        kernel,
        out_shape=shapes,
        in_specs=[hbm, hbm, hbm, hbm, hbm, hbm, hbm, pl.BlockSpec(memory_space=pltpu.SMEM)],
        out_specs=(vmem, hbm, vmem, vmem, vmem),
        scratch_shapes=[
            pltpu.VMEM((ROWS, DT), bf16),
            pltpu.VMEM((DT, DT), bf16),
            pltpu.VMEM((DT, E), bf16),
            pltpu.VMEM((4, 2, 2, 4, 2, 16, E), bf16),
            pltpu.VMEM((ROWS, 128), f32),
            pltpu.VMEM((ROWS, 128), f32),
            pltpu.VMEM((ROWS, 1), f32),
            pltpu.VMEM((CAPS, DT), f32),
            pltpu.VMEM((CAPS, DT), f32),
            pltpu.VMEM((2 * CAPS, DT), bf16),
            pltpu.VMEM((CAPS, DT), bf16),
            pltpu.VMEM((NC, 2, CAPS, 128), bf16),
            pltpu.VMEM((NC, 2, CAPS, 128), bf16),
            pltpu.VMEM((NC, CAPS, PW), bf16),
            pltpu.VMEM((CAPS, DT), bf16),
            pltpu.VMEM((4 * CAPS, DT), bf16),
            pltpu.VMEM((1, ROWS), jnp.int32),
            pltpu.VMEM((1, CAPS), jnp.int32),
            pltpu.VMEM((16, E), bf16),
            pltpu.VMEM((1, DT), f32),
            pltpu.VMEM((ROWS, DT), bf16),
            pltpu.VMEM((GR, E), f32),
            pltpu.VMEM((SLOTS, 512), bf16),
            pltpu.VMEM((GR + CAPS, 512), bf16),
            pltpu.VMEM((GR + CAPS, E), f32),
            pltpu.VMEM((SLOTS, 1), f32),
            pltpu.VMEM((NR, 16, E), bf16),
            pltpu.VMEM((NR, 16, E), bf16),
            pltpu.VMEM((NR, 16, E), bf16),
            pltpu.VMEM((NR, 16, E), bf16),
            pltpu.VMEM((NR, 8, 128), f32),
            pltpu.VMEM((NC, 8, 128), f32),
            dma((5,)),
            dma((DT // TN,)),
            dma((4,)),
            dma((4,)),
            dma((PARTS, 2, 3)),
            dma((PARTS, 2, 3)),
            dma((PARTS, 4, 3)),
            dma((PARTS, 4, 3)),
            dma((PARTS, 4)),
            dma((PARTS, 4)),
            dma((3,)),
            dma((3,)),
            dma((4,)),
            dma((4,)),
            dma((NC - 1,)),
            dma((NC - 1,)),
            dma((NR - 1,)),
            dma((NR - 1,)),
            dma((NR - 1,)),
            dma((NR - 1,)),
            dma((NR - 1,)),
            dma((NR - 1,)),
            dma((NC - 1,)),
            dma((NC - 1,)),
        ],
        compiler_params=pltpu.CompilerParams(
            collective_id=0, has_side_effects=True, vmem_limit_bytes=56 * 1024 * 1024
        ),
    )(tokens, weight, head, segment_ids, owners, images, gain.reshape(1, DT), logit_params)
    loss, d_tokens, d_weight, d_gain, d_images = pl.pallas_call(
        hand_over,
        out_shape=shapes,
        in_specs=[hbm] * 5,
        out_specs=(hbm,) * 5,
        scratch_shapes=[pltpu.VMEM(out.shape, out.dtype) for out in shapes] + [dma((12,)), dma((12,))],
        compiler_params=pltpu.CompilerParams(vmem_limit_bytes=56 * 1024 * 1024),
    )(*held)
    return loss.reshape(16), d_tokens, d_weight, d_gain.reshape(DT), d_images


def solution(mesh):
    rows = P(("blk", "dp"), None)
    return jax.shard_map(
        per_device,
        mesh=mesh,
        in_specs=(rows, rows, rows, rows, P(), P(), P(), P()),
        out_specs=(P(("blk", "dp")), rows, rows, P(), rows),
        check_vma=False,
    )
```

```python
import functools

import jax
import jax.numpy as jnp
from jax import lax
from jax.experimental import pallas as pl
from jax.experimental.pallas import tpu as pltpu
from jax.sharding import PartitionSpec as P

f32 = jnp.float32
bf16 = jnp.bfloat16
MESH = pl.DeviceIdType.MESH

DT = 2048
E = 1152
ROWS = 512
CAPS = 32
NB = 16
ND = 8
TOTAL = 2048
NC = 8
NR = 16
SLOTS = NC * CAPS
GR = NR * 16
PW = E + 128
PARTS = 3
ORDERS = (("x", "y", "z"), ("y", "z", "x"), ("z", "x", "y"))
COLUMNS = ((0, 128), (128, 384), (512, 640))
TN = 512
UNROLL = True


def mm(a, b):
    return lax.dot_general(a, b, (((1,), (0,)), ((), ())), preferred_element_type=f32)


def mm_nt(a, b):
    return lax.dot_general(a, b, (((1,), (1,)), ((), ())), preferred_element_type=f32)


def split2(v):
    hi = v.astype(bf16)
    return hi, (v - hi.astype(f32)).astype(bf16)


def iota(shape, dim):
    return lax.broadcasted_iota(jnp.int32, shape, dim)


def kernel(
    tok_hbm, w_hbm, head_hbm, seg_hbm, own_hbm, img_hbm, gain_hbm, lp_ref,
    loss_out, dtok_hbm, dw_out, dgain_out, dimg_out,
    tok, wv, headv, img, lcol, segt, invc, xs, xp, npst, pooled, asrc, arcv, tbuf, dcap, stack,
    seg_ref, own_ref, img_ref, gain_ref, stage, wh, coefs, zc, bacc, rsacc, c3as, c3ar, c3bs, c3br, gbuf, g2,
    ld_sem, w_sem, in_sem, st_sem,
    i_send, i_recv, j_send, j_recv, ic_send, ic_recv, t_send, t_recv, tc_send, tc_recv, a_send, a_recv,
    ca_send, ca_recv, cb_send, cb_recv, g_send, g_recv, h_send, h_recv,
):
    b = lax.axis_index("blk")
    d = lax.axis_index("dp")
    z, xh, core = b // 4, (b // 2) % 2, b % 2
    y, xl = d // 2, d % 2
    x = xh * 2 + xl
    sib = (b + 1 - 2 * core, d)
    place = z * 2 + core
    seat = xh * ND + d

    here = {"x": x, "y": y, "z": z, "core": core}

    def device(at):
        return (at["z"] * 4 + (at["x"] // 2) * 2 + at["core"], at["y"] * 2 + at["x"] % 2)

    def step_of(axis, n):
        at = dict(here)
        at[axis] = (here[axis] + 4 + n) % 4
        return at

    barrier = pltpu.get_barrier_semaphore()
    pl.semaphore_signal(barrier, inc=1, device_id=sib, device_id_type=MESH)
    for axis in ("x", "y", "z"):
        for k in (1, 3, 2):
            pl.semaphore_signal(barrier, inc=1, device_id=device(step_of(axis, k)), device_id_type=MESH)

    inputs = []
    for i, (src, dst) in enumerate(((img_hbm, img_ref), (seg_hbm, seg_ref), (own_hbm, own_ref), (gain_hbm, gain_ref))):
        cp = pltpu.make_async_copy(src, dst, in_sem.at[i])
        cp.start()
        inputs.append(cp)
    loads = []
    for i in range(4):
        cp = pltpu.make_async_copy(
            tok_hbm.at[pl.ds(i * 128, 128), :], tok.at[pl.ds(i * 128, 128), :], ld_sem.at[i]
        )
        cp.start()
        loads.append(cp)
    wloads = []
    for i in range(DT // TN):
        cp = pltpu.make_async_copy(
            w_hbm.at[:, pl.ds(i * TN, TN)], wv.at[:, pl.ds(i * TN, TN)], w_sem.at[i]
        )
        cp.start()
        wloads.append(cp)
    hload = pltpu.make_async_copy(head_hbm, headv, ld_sem.at[4])
    hload.start()

    inputs[0].wait()
    im = img_ref[...].astype(f32)
    img_inv = lax.rsqrt(jnp.sum(im * im, axis=1, keepdims=True) + 1e-06)
    img_unit = im * img_inv
    img[z, xh, core, y, xl] = img_unit.astype(bf16)

    sends = []

    def region(p, at):
        def pick(name):
            return slice(None) if at[name] is None else at[name]

        xx = at["x"]
        return img.at[
            pick("z"),
            slice(None) if xx is None else xx // 2,
            at["core"],
            pick("y"),
            slice(None) if xx is None else xx % 2,
            :,
            pl.ds(*COLUMNS[p]),
        ]

    def ring_region(p, done, where):
        at = dict(where)
        for name in done:
            at[name] = None
        return region(p, at)

    def ring_copy(p, s, k, where, to):
        ref = ring_region(p, ORDERS[p][:s], where)
        return pltpu.make_async_remote_copy(
            src_ref=ref, dst_ref=ref, send_sem=i_send.at[p, s, k], recv_sem=i_recv.at[p, s, k],
            device_id=device(to), device_id_type=MESH,
        )

    def last_copy(p, j, k, where, to):
        first, second, _ = ORDERS[p]
        at = dict(where)
        at[second] = (here[second] + 4 - j) % 4
        ref = ring_region(p, (first,), at)
        return pltpu.make_async_remote_copy(
            src_ref=ref, dst_ref=ref, send_sem=j_send.at[p, j, k], recv_sem=j_recv.at[p, j, k],
            device_id=device(to), device_id_type=MESH,
        )

    def ring_send(p, s):
        for k in range(3):
            cp = ring_copy(p, s, k, here, step_of(ORDERS[p][s], k + 1))
            cp.start()
            sends.append(cp)

    def ring_wait(p, s, k):
        frm = step_of(ORDERS[p][s], -1 - k)
        ring_copy(p, s, k, frm, frm).wait_recv()

    def last_send(p, j):
        for k in range(3):
            cp = last_copy(p, j, k, here, step_of(ORDERS[p][2], k + 1))
            cp.start()
            sends.append(cp)

    def last_wait(p, k):
        frm = step_of(ORDERS[p][2], -1 - k)
        for j in range(4):
            last_copy(p, j, k, frm, frm).wait_recv()

    def core_copy(p, q, own):
        order = ORDERS[p]
        at = dict(here)
        for name in order[:2]:
            at[name] = None
        if q:
            at[order[2]] = (here[order[2]] + 4 - q) % 4
        if not own:
            at["core"] = 1 - core
        ref = region(p, at)
        return pltpu.make_async_remote_copy(
            src_ref=ref, dst_ref=ref, send_sem=ic_send.at[p, q], recv_sem=ic_recv.at[p, q],
            device_id=sib, device_id_type=MESH,
        )

    def core_send(p, q):
        cp = core_copy(p, q, True)
        cp.start()
        sends.append(cp)

    pl.semaphore_wait(barrier, 10)
    for p in range(PARTS):
        ring_send(p, 0)

    for cp in inputs[1:]:
        cp.wait()
    segf = seg_ref[...].astype(f32)
    segt[...] = jnp.broadcast_to(segf, (128, ROWS)).T
    lane = iota((128, 128), 1)
    cap_of = (lane % CAPS).astype(f32)
    kind = lane // CAPS

    def token_rows(i):
        loads[i].wait()
        rows = pl.ds(i * 128, 128)
        xx = tok[rows, :].astype(f32)
        inv = lax.rsqrt(jnp.sum(xx * xx, axis=1, keepdims=True) * (1.0 / DT) + 1e-06)
        invc[rows, :] = inv
        hi = inv.astype(bf16).astype(f32)
        lo = inv - hi
        val = jnp.where(kind == 0, 1.0, jnp.where(kind == 2, lo, hi))
        lcol[rows, :] = jnp.where(segt[rows, :] == cap_of, val, 0.0)

    for i in range(4):
        token_rows(i)

    lrow = lcol[...].T.astype(bf16)

    def pool_tile(i, _):
        cols = pl.ds(pl.multiple_of(i * TN, TN), TN)
        acc = mm(lrow, tok[:, cols])
        xs[:, cols] = acc[0:CAPS]
        xpt = acc[CAPS : 2 * CAPS] + acc[2 * CAPS : 3 * CAPS]
        xp[:, cols] = xpt
        hi, lo = split2(xpt * gain_ref[:, cols])
        npst[0:CAPS, cols] = hi
        npst[CAPS : 2 * CAPS, cols] = lo
        return 0

    lax.fori_loop(0, DT // TN, pool_tile, 0)

    sel = (jnp.broadcast_to(segf, (CAPS, ROWS)) == iota((CAPS, ROWS), 0).astype(f32)).astype(f32)
    rcount = 1.0 / jnp.maximum(jnp.sum(sel, axis=1, keepdims=True), 1.0)
    ownf = own_ref[...].astype(f32)
    own_col = jnp.sum(
        jnp.where(iota((CAPS, CAPS), 0) == iota((CAPS, CAPS), 1), jnp.broadcast_to(ownf, (CAPS, CAPS)), 0.0),
        axis=1,
        keepdims=True,
    )

    for i in range(DT // TN):
        if i == 2:
            for p in (2, 1, 0):
                for k in range(3):
                    ring_wait(p, 0, k)
                ring_send(p, 1)
            for p in (2, 1, 0):
                last_send(p, 0)
        wloads[i].wait()
        cols = pl.ds(i * TN, TN)
        yy = mm(npst[...], wv[:, cols])
        pooled[:, cols] = ((xs[:, cols] + yy[0:CAPS] + yy[CAPS : 2 * CAPS]) * rcount).astype(bf16)

    hload.wait()
    proj = mm(pooled[...], headv[...])
    scale_inv = lax.rsqrt(jnp.sum(proj * proj, axis=1, keepdims=True) + 1e-06)
    text_unit = proj * scale_inv
    text = text_unit.astype(bf16)
    tbuf[place, :, 0:E] = text
    tbuf[place, :, E:PW] = jnp.broadcast_to(own_col, (CAPS, 128)).astype(bf16)
    factor = scale_inv * rcount
    for j in range(NB):
        cols = pl.ds(j * 128, 128)
        asrc[j // 4 * 2 + j % 2, j // 2 % 2] = (xp[:, cols] * factor).astype(bf16)
    arcv[place] = asrc[place]

    def text_copy(k, idx, to):
        return pltpu.make_async_remote_copy(
            src_ref=tbuf.at[idx], dst_ref=tbuf.at[idx], send_sem=t_send.at[k], recv_sem=t_recv.at[k],
            device_id=device(to), device_id_type=MESH,
        )

    def text_core(k, idx):
        return pltpu.make_async_remote_copy(
            src_ref=tbuf.at[idx], dst_ref=tbuf.at[idx], send_sem=tc_send.at[k], recv_sem=tc_recv.at[k],
            device_id=sib, device_id_type=MESH,
        )

    for k in range(3):
        cp = text_copy(k, place, step_of("z", k + 1))
        cp.start()
        sends.append(cp)
    cp = text_core(3, place)
    cp.start()
    sends.append(cp)
    for p in (2, 1, 0):
        for k in (0, 2, 1):
            ring_wait(p, 1, k)
            last_send(p, k + 1)
    for p in range(PARTS):
        core_send(p, 0)

    def column_peer(k):
        n = (place + k + 1) % NC
        return n, (n // 2 * 4 + xh * 2 + n % 2, d)

    def column_copy(src, dst, k, to, ssem, rsem):
        return pltpu.make_async_remote_copy(
            src_ref=src, dst_ref=dst, send_sem=ssem.at[k], recv_sem=rsem.at[k], device_id=to, device_id_type=MESH
        )

    def column_wait(buf, k, ssem, rsem):
        frm, dev = column_peer(NC - 2 - k)
        column_copy(buf.at[frm], buf.at[frm], k, dev, ssem, rsem).wait_recv()

    for k in range(NC - 1):
        n, to = column_peer(k)
        cp = column_copy(asrc.at[n], arcv.at[place], k, to, a_send, a_recv)
        cp.start()
        sends.append(cp)
    first = pl.multiple_of((z * 4 + core) * 128, 128)
    rows_of = [wv[pl.ds(pl.multiple_of(first + 256 * h, 128), 128), :] for h in range(2)]
    wh[...] = mm(jnp.concatenate(rows_of, axis=0), headv[...])

    for k in (0, 2, 1):
        frm = step_of("z", -1 - k)
        idx = frm["z"] * 2 + core
        text_copy(k, idx, frm).wait_recv()
        cp = text_core(k, idx)
        cp.start()
        sends.append(cp)
    for p in range(PARTS):
        for k in (0, 2, 1):
            last_wait(p, k)
            core_send(p, k + 1)
    for p in range(PARTS):
        for q in range(4):
            core_copy(p, q, False).wait_recv()

    scale = jnp.exp(jnp.full((1, 128), lp_ref[0], f32))[:, 0:1]
    bias = jnp.full((1, 128), lp_ref[1], f32)[:, 0:1]

    def pair(dots, gid, ids):
        val = scale * dots + bias
        same = gid == ids
        arg = jnp.where(same, -val, val)
        coef = jnp.where(same, -scale, scale) * pl.reciprocal(1.0 + jnp.exp(-arg), approx=True)
        return arg, coef

    def row_copy(src, dst, k, ssem, rsem):
        n = (seat + k + 1) % NR
        return pltpu.make_async_remote_copy(
            src_ref=src, dst_ref=dst, send_sem=ssem.at[k], recv_sem=rsem.at[k],
            device_id=(z * 4 + n // ND * 2 + core, n % ND), device_id_type=MESH,
        )

    def row_wait(buf, k, ssem, rsem):
        frm = (seat + NR - 1 - k) % NR
        row_copy(buf.at[frm], buf.at[frm], k, ssem, rsem).wait_recv()

    for k in (0, 2, 1):
        text_core(k, step_of("z", -1 - k)["z"] * 2 + 1 - core).wait_recv()
    text_core(3, place + 1 - 2 * core).wait_recv()

    owner = tbuf[:, :, E:PW].reshape(SLOTS, 128).astype(f32)[:, 0:1]
    row = iota((SLOTS, 1), 0) // CAPS
    block = ((row // 2 * 4 + row % 2 + xh * 2) * 128).astype(f32)
    gid = jnp.where(owner >= 0.0, owner + block, -1.0)
    texts = tbuf[:, :, 0:E].reshape(SLOTS, E)
    group = img[z, :, core].reshape(GR, E)
    lane_g = iota((1, GR), 1)
    ids_g = ((z * 4 + core) * 128 + lane_g + lane_g // 128 * 128).astype(f32)
    arg, coef = pair(mm_nt(texts, group), gid, ids_g)
    dimg_part = mm(coef.T.astype(bf16), texts)
    c3as[...] = dimg_part.reshape(NR, 16, E).astype(bf16)
    c3ar[seat] = c3as[seat]
    for k in range(NR - 1):
        cp = row_copy(c3as.at[(seat + k + 1) % NR], c3ar.at[seat], k, ca_send, ca_recv)
        cp.start()
        sends.append(cp)
    soft = jnp.maximum(arg, 0.0) + jnp.log1p(jnp.exp(-jnp.abs(arg)))
    loss_part = jnp.sum(jnp.where(gid >= 0.0, soft, 0.0), axis=0, keepdims=True)

    for k in range(NC - 1):
        column_wait(arcv, k, a_send, a_recv)
    share = jnp.concatenate([arcv[:, h].reshape(SLOTS, 128) for h in range(2)], axis=1).astype(f32)
    share_t = share.T.astype(bf16)
    bacc[...] = jnp.zeros((GR + CAPS, E), f32)
    rsacc[...] = jnp.zeros((SLOTS, 1), f32)

    def pair_chunk(c, _):
        chunk = img[c].reshape(512, E)
        dots = mm_nt(tbuf[:, :, 0:E].reshape(SLOTS, E), chunk)
        _, coef = pair(dots, gid, (iota((1, 512), 1) + c * 512).astype(f32))
        rsacc[...] += jnp.sum(coef * dots, axis=1, keepdims=True)
        coefs[...] = coef.astype(bf16)
        zc[0:GR, :] = mm(share_t, coefs[...]).astype(bf16)
        zc[GR : GR + CAPS, :] = coefs[pl.ds(pl.multiple_of(place * CAPS, CAPS), CAPS), :]
        bacc[...] += mm(zc[...], chunk)
        return 0

    lax.fori_loop(0, 4, pair_chunk, 0, unroll=UNROLL)

    minus_t = (share * rsacc[...]).T.astype(bf16)
    bpart = bacc[0:GR, :] - mm(minus_t, texts)
    c3bs[...] = bpart.reshape(NR, 16, E).astype(bf16)
    c3br[seat] = c3bs[seat]
    gain_part = jnp.broadcast_to(jnp.sum(bpart * wh[...], axis=1, keepdims=True), (GR, 128)).T[0:1]
    gbuf[seat] = jnp.zeros((8, 128), f32)
    for h in range(2):
        gbuf[seat, h : h + 1, :] = loss_part[:, 128 * h : 128 * h + 128]
        gbuf[seat, 2 + h : 3 + h, :] = gain_part[:, 128 * h : 128 * h + 128]
    for k in range(NR - 1):
        cp = row_copy(gbuf.at[seat], gbuf.at[seat], k, g_send, g_recv)
        cp.start()
        sends.append(cp)
    for k in range(NR - 1):
        cp = row_copy(c3bs.at[(seat + k + 1) % NR], c3br.at[seat], k, cb_send, cb_recv)
        cp.start()
        sends.append(cp)

    dtext = bacc[GR : GR + CAPS, :]
    dproj = (
        scale_inv * (dtext - text_unit * jnp.sum(text_unit * dtext, axis=1, keepdims=True))
    ).astype(bf16)
    live = jnp.where(own_col >= 0.0, rcount, 0.0)

    def dcap_tile(i, _):
        rows = pl.ds(pl.multiple_of(i * TN, TN), TN)
        dpool = mm_nt(dproj, headv[rows, :]).astype(bf16).astype(f32)
        dc = (dpool * live).astype(bf16)
        dcap[:, rows] = dc
        stack[0:CAPS, rows] = dc
        return 0

    lax.fori_loop(0, DT // TN, dcap_tile, 0, unroll=True)

    def dnorm_tile(i, _):
        rows = pl.ds(pl.multiple_of(i * TN, TN), TN)
        hi, lo = split2(mm_nt(dcap[...], wv[rows, :]) * gain_ref[:, rows])
        stack[CAPS : 2 * CAPS, rows] = hi
        stack[2 * CAPS : 3 * CAPS, rows] = hi
        stack[3 * CAPS : 4 * CAPS, rows] = lo
        return 0

    lax.fori_loop(0, DT // TN, dnorm_tile, 0, unroll=True)

    for k in range(NR - 1):
        row_wait(gbuf, k, g_send, g_recv)
    gsum = jnp.sum(gbuf[...], axis=0)
    g2[place] = gsum
    for k in range(NC - 1):
        _, to = column_peer(k)
        cp = column_copy(g2.at[place], g2.at[place], k, to, h_send, h_recv)
        cp.start()
        sends.append(cp)

    stores = []
    for i in range(4):
        rows = pl.ds(i * 128, 128)
        xb = tok[rows, :]
        lc = lcol[rows, :]
        q = mm_nt(xb, stack[...])
        mine = (segt[rows, :] == cap_of) & ((kind == 1) | (kind == 3))
        mean = jnp.sum(jnp.where(mine, q, 0.0), axis=1, keepdims=True) * (1.0 / DT)
        inv = invc[rows, :]
        drop = inv * inv * inv * mean
        full = mm(lc.astype(bf16), stack[...])
        stage[rows, :] = (full - xb.astype(f32) * drop).astype(bf16)
        cp = pltpu.make_async_copy(stage.at[rows, :], dtok_hbm.at[rows, :], st_sem.at[i])
        cp.start()
        stores.append(cp)

    for k in range(NR - 1):
        row_wait(c3ar, k, ca_send, ca_recv)
    dimg = jnp.sum(c3ar[...].astype(f32), axis=0)
    dimg_out[...] = img_inv * (dimg - img_unit * jnp.sum(img_unit * dimg, axis=1, keepdims=True))
    for k in range(NR - 1):
        row_wait(c3br, k, cb_send, cb_recv)
    mine = iota((16, 128), 1) == iota((16, 128), 0) + 16 * d

    def own_rows(row):
        return jnp.sum(jnp.where(mine, jnp.broadcast_to(row, (16, 128)), 0.0), axis=1, keepdims=True)

    gain_col = own_rows(gain_ref[:, pl.ds(pl.multiple_of(b * 128, 128), 128)])
    hi, lo = split2(jnp.sum(c3br[...].astype(f32), axis=0) * gain_col)
    both = jnp.concatenate([hi, lo], axis=0)

    def dw_tile(i, _):
        rows = pl.ds(pl.multiple_of(i * TN, TN), TN)
        dw = mm_nt(both, headv[rows, :])
        dw_out[:, rows] = dw[0:16] + dw[16:32]
        return 0

    lax.fori_loop(0, DT // TN, dw_tile, 0, unroll=True)

    col = own_rows(jnp.where(xh == 0, gsum[0:1], gsum[1:2]) * (1.0 / TOTAL))
    loss_out[...] = jnp.sum(jnp.where(iota((16, 16), 0) == iota((16, 16), 1), col, 0.0), axis=0, keepdims=True)

    for k in range(NC - 1):
        column_wait(g2, k, h_send, h_recv)
    for r in range(NB):
        h = r // 2 % 2
        dgain_out[r : r + 1, :] = g2[r // 4 * 2 + r % 2, 2 + h : 3 + h, :]

    for cp in stores:
        cp.wait()
    for cp in sends:
        cp.wait_send()


def hand_over(
    loss, dtok, dw, dgain, dimg, loss_out, dtok_out, dw_out, dgain_out, dimg_out,
    loss_buf, dtok_buf, dw_buf, dgain_buf, dimg_buf, ins, outs,
):
    trips = [
        (dtok.at[rows, :], dtok_buf.at[rows, :], dtok_out.at[rows, :])
        for rows in [pl.ds(i * 64, 64) for i in range(8)]
    ]
    trips += [
        (dw, dw_buf, dw_out), (dimg, dimg_buf, dimg_out), (dgain, dgain_buf, dgain_out), (loss, loss_buf, loss_out)
    ]
    reads, writes = [], []
    for i, (src, buf, _) in enumerate(trips):
        cp = pltpu.make_async_copy(src, buf, ins.at[i])
        cp.start()
        reads.append(cp)
    for i, (_, buf, dst) in enumerate(trips):
        reads[i].wait()
        cp = pltpu.make_async_copy(buf, dst, outs.at[i])
        cp.start()
        writes.append(cp)
    for cp in writes:
        cp.wait()


def per_device(tokens, segment_ids, owners, images, weight, gain, head, logit_params):
    vmem = pl.BlockSpec(memory_space=pltpu.VMEM)
    hbm = pl.BlockSpec(memory_space=pl.ANY)
    dma = pltpu.SemaphoreType.DMA
    shapes = (
        jax.ShapeDtypeStruct((1, 16), f32),
        jax.ShapeDtypeStruct((ROWS, DT), bf16),
        jax.ShapeDtypeStruct((16, DT), f32),
        jax.ShapeDtypeStruct((16, 128), f32),
        jax.ShapeDtypeStruct((16, E), f32),
    )
    held = pl.pallas_call(
        kernel,
        out_shape=shapes,
        in_specs=[hbm, hbm, hbm, hbm, hbm, hbm, hbm, pl.BlockSpec(memory_space=pltpu.SMEM)],
        out_specs=(vmem, hbm, vmem, vmem, vmem),
        scratch_shapes=[
            pltpu.VMEM((ROWS, DT), bf16),
            pltpu.VMEM((DT, DT), bf16),
            pltpu.VMEM((DT, E), bf16),
            pltpu.VMEM((4, 2, 2, 4, 2, 16, E), bf16),
            pltpu.VMEM((ROWS, 128), f32),
            pltpu.VMEM((ROWS, 128), f32),
            pltpu.VMEM((ROWS, 1), f32),
            pltpu.VMEM((CAPS, DT), f32),
            pltpu.VMEM((CAPS, DT), f32),
            pltpu.VMEM((2 * CAPS, DT), bf16),
            pltpu.VMEM((CAPS, DT), bf16),
            pltpu.VMEM((NC, 2, CAPS, 128), bf16),
            pltpu.VMEM((NC, 2, CAPS, 128), bf16),
            pltpu.VMEM((NC, CAPS, PW), bf16),
            pltpu.VMEM((CAPS, DT), bf16),
            pltpu.VMEM((4 * CAPS, DT), bf16),
            pltpu.VMEM((1, ROWS), jnp.int32),
            pltpu.VMEM((1, CAPS), jnp.int32),
            pltpu.VMEM((16, E), bf16),
            pltpu.VMEM((1, DT), f32),
            pltpu.VMEM((ROWS, DT), bf16),
            pltpu.VMEM((GR, E), f32),
            pltpu.VMEM((SLOTS, 512), bf16),
            pltpu.VMEM((GR + CAPS, 512), bf16),
            pltpu.VMEM((GR + CAPS, E), f32),
            pltpu.VMEM((SLOTS, 1), f32),
            pltpu.VMEM((NR, 16, E), bf16),
            pltpu.VMEM((NR, 16, E), bf16),
            pltpu.VMEM((NR, 16, E), bf16),
            pltpu.VMEM((NR, 16, E), bf16),
            pltpu.VMEM((NR, 8, 128), f32),
            pltpu.VMEM((NC, 8, 128), f32),
            dma((5,)),
            dma((DT // TN,)),
            dma((4,)),
            dma((4,)),
            dma((PARTS, 2, 3)),
            dma((PARTS, 2, 3)),
            dma((PARTS, 4, 3)),
            dma((PARTS, 4, 3)),
            dma((PARTS, 4)),
            dma((PARTS, 4)),
            dma((3,)),
            dma((3,)),
            dma((4,)),
            dma((4,)),
            dma((NC - 1,)),
            dma((NC - 1,)),
            dma((NR - 1,)),
            dma((NR - 1,)),
            dma((NR - 1,)),
            dma((NR - 1,)),
            dma((NR - 1,)),
            dma((NR - 1,)),
            dma((NC - 1,)),
            dma((NC - 1,)),
        ],
        compiler_params=pltpu.CompilerParams(
            collective_id=0, has_side_effects=True, vmem_limit_bytes=56 * 1024 * 1024
        ),
    )(tokens, weight, head, segment_ids, owners, images, gain.reshape(1, DT), logit_params)
    loss, d_tokens, d_weight, d_gain, d_images = pl.pallas_call(
        hand_over,
        out_shape=shapes,
        in_specs=[hbm] * 5,
        out_specs=(hbm,) * 5,
        scratch_shapes=[pltpu.VMEM(out.shape, out.dtype) for out in shapes] + [dma((12,)), dma((12,))],
        compiler_params=pltpu.CompilerParams(vmem_limit_bytes=56 * 1024 * 1024),
    )(*held)
    return loss.reshape(16), d_tokens, d_weight, d_gain.reshape(DT), d_images


def solution(mesh):
    rows = P(("blk", "dp"), None)
    return jax.shard_map(
        per_device,
        mesh=mesh,
        in_specs=(rows, rows, rows, rows, P(), P(), P(), P()),
        out_specs=(P(("blk", "dp")), rows, rows, P(), rows),
        check_vma=False,
    )
```

```python
import functools

import jax
import jax.numpy as jnp
from jax import lax
from jax.experimental import pallas as pl
from jax.experimental.pallas import tpu as pltpu
from jax.sharding import PartitionSpec as P

f32 = jnp.float32
bf16 = jnp.bfloat16
MESH = pl.DeviceIdType.MESH

DT = 2048
E = 1152
ROWS = 512
CAPS = 32
NB = 16
ND = 8
TOTAL = 2048
NC = 8
NR = 16
SLOTS = NC * CAPS
GR = NR * 16
PW = E + 128
PARTS = 3
ORDERS = (("x", "y", "z"), ("y", "z", "x"), ("z", "x", "y"))
COLUMNS = ((0, 128), (128, 384), (512, 640))
TN = 512
UNROLL = True


def mm(a, b):
    return lax.dot_general(a, b, (((1,), (0,)), ((), ())), preferred_element_type=f32)


def mm_nt(a, b):
    return lax.dot_general(a, b, (((1,), (1,)), ((), ())), preferred_element_type=f32)


def split2(v):
    hi = v.astype(bf16)
    return hi, (v - hi.astype(f32)).astype(bf16)


def iota(shape, dim):
    return lax.broadcasted_iota(jnp.int32, shape, dim)


def kernel(
    tok_hbm, w_hbm, head_hbm, seg_hbm, own_hbm, img_hbm, gain_hbm, lp_ref,
    loss_out, dtok_hbm, dw_hbm, dgain_out, dimg_hbm,
    tok, wv, headv, img, lcol, segt, invc, xs, xp, npst, pooled, asrc, arcv, tbuf, dcap, stack,
    seg_ref, own_ref, img_ref, gain_ref, dw_buf, dimg_buf, stage, wh, coefs, zc, bacc, rsacc, c3as, c3ar, c3bs, c3br, gbuf, g2,
    ld_sem, w_sem, in_sem, st_sem, out_sem,
    i_send, i_recv, j_send, j_recv, ic_send, ic_recv, t_send, t_recv, tc_send, tc_recv, a_send, a_recv,
    ca_send, ca_recv, cb_send, cb_recv, g_send, g_recv, h_send, h_recv,
):
    b = lax.axis_index("blk")
    d = lax.axis_index("dp")
    z, xh, core = b // 4, (b // 2) % 2, b % 2
    y, xl = d // 2, d % 2
    x = xh * 2 + xl
    sib = (b + 1 - 2 * core, d)
    place = z * 2 + core
    seat = xh * ND + d

    here = {"x": x, "y": y, "z": z, "core": core}

    def device(at):
        return (at["z"] * 4 + (at["x"] // 2) * 2 + at["core"], at["y"] * 2 + at["x"] % 2)

    def step_of(axis, n):
        at = dict(here)
        at[axis] = (here[axis] + 4 + n) % 4
        return at

    barrier = pltpu.get_barrier_semaphore()
    pl.semaphore_signal(barrier, inc=1, device_id=sib, device_id_type=MESH)
    for axis in ("x", "y", "z"):
        for k in (1, 3, 2):
            pl.semaphore_signal(barrier, inc=1, device_id=device(step_of(axis, k)), device_id_type=MESH)

    inputs = []
    for i, (src, dst) in enumerate(((img_hbm, img_ref), (seg_hbm, seg_ref), (own_hbm, own_ref), (gain_hbm, gain_ref))):
        cp = pltpu.make_async_copy(src, dst, in_sem.at[i])
        cp.start()
        inputs.append(cp)
    loads = []
    for i in range(4):
        cp = pltpu.make_async_copy(
            tok_hbm.at[pl.ds(i * 128, 128), :], tok.at[pl.ds(i * 128, 128), :], ld_sem.at[i]
        )
        cp.start()
        loads.append(cp)
    wloads = []
    for i in range(DT // TN):
        cp = pltpu.make_async_copy(
            w_hbm.at[:, pl.ds(i * TN, TN)], wv.at[:, pl.ds(i * TN, TN)], w_sem.at[i]
        )
        cp.start()
        wloads.append(cp)
    hload = pltpu.make_async_copy(head_hbm, headv, ld_sem.at[4])
    hload.start()

    inputs[0].wait()
    im = img_ref[...].astype(f32)
    img_inv = lax.rsqrt(jnp.sum(im * im, axis=1, keepdims=True) + 1e-06)
    img_unit = im * img_inv
    img[z, xh, core, y, xl] = img_unit.astype(bf16)

    sends = []

    def region(p, at):
        def pick(name):
            return slice(None) if at[name] is None else at[name]

        xx = at["x"]
        return img.at[
            pick("z"),
            slice(None) if xx is None else xx // 2,
            at["core"],
            pick("y"),
            slice(None) if xx is None else xx % 2,
            :,
            pl.ds(*COLUMNS[p]),
        ]

    def ring_region(p, done, where):
        at = dict(where)
        for name in done:
            at[name] = None
        return region(p, at)

    def ring_copy(p, s, k, where, to):
        ref = ring_region(p, ORDERS[p][:s], where)
        return pltpu.make_async_remote_copy(
            src_ref=ref, dst_ref=ref, send_sem=i_send.at[p, s, k], recv_sem=i_recv.at[p, s, k],
            device_id=device(to), device_id_type=MESH,
        )

    def last_copy(p, j, k, where, to):
        first, second, _ = ORDERS[p]
        at = dict(where)
        at[second] = (here[second] + 4 - j) % 4
        ref = ring_region(p, (first,), at)
        return pltpu.make_async_remote_copy(
            src_ref=ref, dst_ref=ref, send_sem=j_send.at[p, j, k], recv_sem=j_recv.at[p, j, k],
            device_id=device(to), device_id_type=MESH,
        )

    def ring_send(p, s):
        for k in range(3):
            cp = ring_copy(p, s, k, here, step_of(ORDERS[p][s], k + 1))
            cp.start()
            sends.append(cp)

    def ring_wait(p, s, k):
        frm = step_of(ORDERS[p][s], -1 - k)
        ring_copy(p, s, k, frm, frm).wait_recv()

    def last_send(p, j):
        for k in range(3):
            cp = last_copy(p, j, k, here, step_of(ORDERS[p][2], k + 1))
            cp.start()
            sends.append(cp)

    def last_wait(p, k):
        frm = step_of(ORDERS[p][2], -1 - k)
        for j in range(4):
            last_copy(p, j, k, frm, frm).wait_recv()

    def core_copy(p, q, own):
        order = ORDERS[p]
        at = dict(here)
        for name in order[:2]:
            at[name] = None
        if q:
            at[order[2]] = (here[order[2]] + 4 - q) % 4
        if not own:
            at["core"] = 1 - core
        ref = region(p, at)
        return pltpu.make_async_remote_copy(
            src_ref=ref, dst_ref=ref, send_sem=ic_send.at[p, q], recv_sem=ic_recv.at[p, q],
            device_id=sib, device_id_type=MESH,
        )

    def core_send(p, q):
        cp = core_copy(p, q, True)
        cp.start()
        sends.append(cp)

    pl.semaphore_wait(barrier, 10)
    for p in range(PARTS):
        ring_send(p, 0)

    for cp in inputs[1:]:
        cp.wait()
    segf = seg_ref[...].astype(f32)
    segt[...] = jnp.broadcast_to(segf, (128, ROWS)).T
    lane = iota((128, 128), 1)
    cap_of = (lane % CAPS).astype(f32)
    kind = lane // CAPS

    def token_rows(i):
        loads[i].wait()
        rows = pl.ds(i * 128, 128)
        xx = tok[rows, :].astype(f32)
        inv = lax.rsqrt(jnp.sum(xx * xx, axis=1, keepdims=True) * (1.0 / DT) + 1e-06)
        invc[rows, :] = inv
        hi = inv.astype(bf16).astype(f32)
        lo = inv - hi
        val = jnp.where(kind == 0, 1.0, jnp.where(kind == 2, lo, hi))
        lcol[rows, :] = jnp.where(segt[rows, :] == cap_of, val, 0.0)

    for i in range(4):
        token_rows(i)

    lrow = lcol[...].T.astype(bf16)

    def pool_tile(i, _):
        cols = pl.ds(pl.multiple_of(i * TN, TN), TN)
        acc = mm(lrow, tok[:, cols])
        xs[:, cols] = acc[0:CAPS]
        xpt = acc[CAPS : 2 * CAPS] + acc[2 * CAPS : 3 * CAPS]
        xp[:, cols] = xpt
        hi, lo = split2(xpt * gain_ref[:, cols])
        npst[0:CAPS, cols] = hi
        npst[CAPS : 2 * CAPS, cols] = lo
        return 0

    lax.fori_loop(0, DT // TN, pool_tile, 0)

    sel = (jnp.broadcast_to(segf, (CAPS, ROWS)) == iota((CAPS, ROWS), 0).astype(f32)).astype(f32)
    rcount = 1.0 / jnp.maximum(jnp.sum(sel, axis=1, keepdims=True), 1.0)
    ownf = own_ref[...].astype(f32)
    own_col = jnp.sum(
        jnp.where(iota((CAPS, CAPS), 0) == iota((CAPS, CAPS), 1), jnp.broadcast_to(ownf, (CAPS, CAPS)), 0.0),
        axis=1,
        keepdims=True,
    )

    for i in range(DT // TN):
        if i == 2:
            for p in (2, 1, 0):
                for k in range(3):
                    ring_wait(p, 0, k)
                ring_send(p, 1)
            for p in (2, 1, 0):
                last_send(p, 0)
        wloads[i].wait()
        cols = pl.ds(i * TN, TN)
        yy = mm(npst[...], wv[:, cols])
        pooled[:, cols] = ((xs[:, cols] + yy[0:CAPS] + yy[CAPS : 2 * CAPS]) * rcount).astype(bf16)

    hload.wait()
    proj = mm(pooled[...], headv[...])
    scale_inv = lax.rsqrt(jnp.sum(proj * proj, axis=1, keepdims=True) + 1e-06)
    text_unit = proj * scale_inv
    text = text_unit.astype(bf16)
    tbuf[place, :, 0:E] = text
    tbuf[place, :, E:PW] = jnp.broadcast_to(own_col, (CAPS, 128)).astype(bf16)
    factor = scale_inv * rcount
    for j in range(NB):
        cols = pl.ds(j * 128, 128)
        asrc[j // 4 * 2 + j % 2, j // 2 % 2] = (xp[:, cols] * factor).astype(bf16)
    arcv[place] = asrc[place]

    def text_copy(k, idx, to):
        return pltpu.make_async_remote_copy(
            src_ref=tbuf.at[idx], dst_ref=tbuf.at[idx], send_sem=t_send.at[k], recv_sem=t_recv.at[k],
            device_id=device(to), device_id_type=MESH,
        )

    def text_core(k, idx):
        return pltpu.make_async_remote_copy(
            src_ref=tbuf.at[idx], dst_ref=tbuf.at[idx], send_sem=tc_send.at[k], recv_sem=tc_recv.at[k],
            device_id=sib, device_id_type=MESH,
        )

    for k in range(3):
        cp = text_copy(k, place, step_of("z", k + 1))
        cp.start()
        sends.append(cp)
    cp = text_core(3, place)
    cp.start()
    sends.append(cp)
    for p in (2, 1, 0):
        for k in (0, 2, 1):
            ring_wait(p, 1, k)
            last_send(p, k + 1)
    for p in range(PARTS):
        core_send(p, 0)

    def column_peer(k):
        n = (place + k + 1) % NC
        return n, (n // 2 * 4 + xh * 2 + n % 2, d)

    def column_copy(src, dst, k, to, ssem, rsem):
        return pltpu.make_async_remote_copy(
            src_ref=src, dst_ref=dst, send_sem=ssem.at[k], recv_sem=rsem.at[k], device_id=to, device_id_type=MESH
        )

    def column_wait(buf, k, ssem, rsem):
        frm, dev = column_peer(NC - 2 - k)
        column_copy(buf.at[frm], buf.at[frm], k, dev, ssem, rsem).wait_recv()

    for k in range(NC - 1):
        n, to = column_peer(k)
        cp = column_copy(asrc.at[n], arcv.at[place], k, to, a_send, a_recv)
        cp.start()
        sends.append(cp)
    first = pl.multiple_of((z * 4 + core) * 128, 128)
    rows_of = [wv[pl.ds(pl.multiple_of(first + 256 * h, 128), 128), :] for h in range(2)]
    wh[...] = mm(jnp.concatenate(rows_of, axis=0), headv[...])

    for k in (0, 2, 1):
        frm = step_of("z", -1 - k)
        idx = frm["z"] * 2 + core
        text_copy(k, idx, frm).wait_recv()
        cp = text_core(k, idx)
        cp.start()
        sends.append(cp)
    for p in range(PARTS):
        for k in (0, 2, 1):
            last_wait(p, k)
            core_send(p, k + 1)
    for p in range(PARTS):
        for q in range(4):
            core_copy(p, q, False).wait_recv()

    scale = jnp.exp(jnp.full((1, 128), lp_ref[0], f32))[:, 0:1]
    bias = jnp.full((1, 128), lp_ref[1], f32)[:, 0:1]

    def pair(dots, gid, ids):
        val = scale * dots + bias
        same = gid == ids
        arg = jnp.where(same, -val, val)
        coef = jnp.where(same, -scale, scale) * pl.reciprocal(1.0 + jnp.exp(-arg), approx=True)
        return arg, coef

    def row_copy(src, dst, k, ssem, rsem):
        n = (seat + k + 1) % NR
        return pltpu.make_async_remote_copy(
            src_ref=src, dst_ref=dst, send_sem=ssem.at[k], recv_sem=rsem.at[k],
            device_id=(z * 4 + n // ND * 2 + core, n % ND), device_id_type=MESH,
        )

    def row_wait(buf, k, ssem, rsem):
        frm = (seat + NR - 1 - k) % NR
        row_copy(buf.at[frm], buf.at[frm], k, ssem, rsem).wait_recv()

    for k in (0, 2, 1):
        text_core(k, step_of("z", -1 - k)["z"] * 2 + 1 - core).wait_recv()
    text_core(3, place + 1 - 2 * core).wait_recv()

    owner = tbuf[:, :, E:PW].reshape(SLOTS, 128).astype(f32)[:, 0:1]
    row = iota((SLOTS, 1), 0) // CAPS
    block = ((row // 2 * 4 + row % 2 + xh * 2) * 128).astype(f32)
    gid = jnp.where(owner >= 0.0, owner + block, -1.0)
    texts = tbuf[:, :, 0:E].reshape(SLOTS, E)
    group = img[z, :, core].reshape(GR, E)
    lane_g = iota((1, GR), 1)
    ids_g = ((z * 4 + core) * 128 + lane_g + lane_g // 128 * 128).astype(f32)
    arg, coef = pair(mm_nt(texts, group), gid, ids_g)
    dimg_part = mm(coef.T.astype(bf16), texts)
    c3as[...] = dimg_part.reshape(NR, 16, E).astype(bf16)
    c3ar[seat] = c3as[seat]
    for k in range(NR - 1):
        cp = row_copy(c3as.at[(seat + k + 1) % NR], c3ar.at[seat], k, ca_send, ca_recv)
        cp.start()
        sends.append(cp)
    soft = jnp.maximum(arg, 0.0) + jnp.log1p(jnp.exp(-jnp.abs(arg)))
    loss_part = jnp.sum(jnp.where(gid >= 0.0, soft, 0.0), axis=0, keepdims=True)

    for k in range(NC - 1):
        column_wait(arcv, k, a_send, a_recv)
    share = jnp.concatenate([arcv[:, h].reshape(SLOTS, 128) for h in range(2)], axis=1).astype(f32)
    share_t = share.T.astype(bf16)
    bacc[...] = jnp.zeros((GR + CAPS, E), f32)
    rsacc[...] = jnp.zeros((SLOTS, 1), f32)

    def pair_chunk(c, _):
        chunk = img[c].reshape(512, E)
        dots = mm_nt(tbuf[:, :, 0:E].reshape(SLOTS, E), chunk)
        _, coef = pair(dots, gid, (iota((1, 512), 1) + c * 512).astype(f32))
        rsacc[...] += jnp.sum(coef * dots, axis=1, keepdims=True)
        coefs[...] = coef.astype(bf16)
        zc[0:GR, :] = mm(share_t, coefs[...]).astype(bf16)
        zc[GR : GR + CAPS, :] = coefs[pl.ds(pl.multiple_of(place * CAPS, CAPS), CAPS), :]
        bacc[...] += mm(zc[...], chunk)
        return 0

    lax.fori_loop(0, 4, pair_chunk, 0, unroll=UNROLL)

    minus_t = (share * rsacc[...]).T.astype(bf16)
    bpart = bacc[0:GR, :] - mm(minus_t, texts)
    c3bs[...] = bpart.reshape(NR, 16, E).astype(bf16)
    c3br[seat] = c3bs[seat]
    gain_part = jnp.broadcast_to(jnp.sum(bpart * wh[...], axis=1, keepdims=True), (GR, 128)).T[0:1]
    gbuf[seat] = jnp.zeros((8, 128), f32)
    for h in range(2):
        gbuf[seat, h : h + 1, :] = loss_part[:, 128 * h : 128 * h + 128]
        gbuf[seat, 2 + h : 3 + h, :] = gain_part[:, 128 * h : 128 * h + 128]
    for k in range(NR - 1):
        cp = row_copy(gbuf.at[seat], gbuf.at[seat], k, g_send, g_recv)
        cp.start()
        sends.append(cp)
    for k in range(NR - 1):
        cp = row_copy(c3bs.at[(seat + k + 1) % NR], c3br.at[seat], k, cb_send, cb_recv)
        cp.start()
        sends.append(cp)

    dtext = bacc[GR : GR + CAPS, :]
    dproj = (
        scale_inv * (dtext - text_unit * jnp.sum(text_unit * dtext, axis=1, keepdims=True))
    ).astype(bf16)
    live = jnp.where(own_col >= 0.0, rcount, 0.0)

    def dcap_tile(i, _):
        rows = pl.ds(pl.multiple_of(i * TN, TN), TN)
        dpool = mm_nt(dproj, headv[rows, :]).astype(bf16).astype(f32)
        dc = (dpool * live).astype(bf16)
        dcap[:, rows] = dc
        stack[0:CAPS, rows] = dc
        return 0

    lax.fori_loop(0, DT // TN, dcap_tile, 0, unroll=True)

    def dnorm_tile(i, _):
        rows = pl.ds(pl.multiple_of(i * TN, TN), TN)
        hi, lo = split2(mm_nt(dcap[...], wv[rows, :]) * gain_ref[:, rows])
        stack[CAPS : 2 * CAPS, rows] = hi
        stack[2 * CAPS : 3 * CAPS, rows] = hi
        stack[3 * CAPS : 4 * CAPS, rows] = lo
        return 0

    lax.fori_loop(0, DT // TN, dnorm_tile, 0, unroll=True)

    for k in range(NR - 1):
        row_wait(gbuf, k, g_send, g_recv)
    gsum = jnp.sum(gbuf[...], axis=0)
    g2[place] = gsum
    for k in range(NC - 1):
        _, to = column_peer(k)
        cp = column_copy(g2.at[place], g2.at[place], k, to, h_send, h_recv)
        cp.start()
        sends.append(cp)

    stores = []
    for i in range(4):
        rows = pl.ds(i * 128, 128)
        xb = tok[rows, :]
        lc = lcol[rows, :]
        q = mm_nt(xb, stack[...])
        mine = (segt[rows, :] == cap_of) & ((kind == 1) | (kind == 3))
        mean = jnp.sum(jnp.where(mine, q, 0.0), axis=1, keepdims=True) * (1.0 / DT)
        inv = invc[rows, :]
        drop = inv * inv * inv * mean
        full = mm(lc.astype(bf16), stack[...])
        stage[rows, :] = (full - xb.astype(f32) * drop).astype(bf16)
        cp = pltpu.make_async_copy(stage.at[rows, :], dtok_hbm.at[rows, :], st_sem.at[i])
        cp.start()
        stores.append(cp)

    for k in range(NR - 1):
        row_wait(c3ar, k, ca_send, ca_recv)
    dimg = jnp.sum(c3ar[...].astype(f32), axis=0)
    dimg_buf[...] = img_inv * (dimg - img_unit * jnp.sum(img_unit * dimg, axis=1, keepdims=True))
    cp = pltpu.make_async_copy(dimg_buf, dimg_hbm, out_sem.at[DT // TN])
    cp.start()
    stores.append(cp)
    for k in range(NR - 1):
        row_wait(c3br, k, cb_send, cb_recv)
    mine = iota((16, 128), 1) == iota((16, 128), 0) + 16 * d

    def own_rows(row):
        return jnp.sum(jnp.where(mine, jnp.broadcast_to(row, (16, 128)), 0.0), axis=1, keepdims=True)

    gain_col = own_rows(gain_ref[:, pl.ds(pl.multiple_of(b * 128, 128), 128)])
    hi, lo = split2(jnp.sum(c3br[...].astype(f32), axis=0) * gain_col)
    both = jnp.concatenate([hi, lo], axis=0)

    for i in range(DT // TN):
        rows = pl.ds(i * TN, TN)
        dw = mm_nt(both, headv[rows, :])
        dw_buf[:, rows] = dw[0:16] + dw[16:32]
        cp = pltpu.make_async_copy(dw_buf.at[:, rows], dw_hbm.at[:, rows], out_sem.at[i])
        cp.start()
        stores.append(cp)

    col = own_rows(jnp.where(xh == 0, gsum[0:1], gsum[1:2]) * (1.0 / TOTAL))
    loss_out[...] = jnp.sum(jnp.where(iota((16, 16), 0) == iota((16, 16), 1), col, 0.0), axis=0, keepdims=True)

    for k in range(NC - 1):
        column_wait(g2, k, h_send, h_recv)
    for r in range(NB):
        h = r // 2 % 2
        dgain_out[r : r + 1, :] = g2[r // 4 * 2 + r % 2, 2 + h : 3 + h, :]

    for cp in stores:
        cp.wait()
    for cp in sends:
        cp.wait_send()


def hand_over(
    loss, dtok, dw, dgain, dimg, loss_out, dtok_out, dw_out, dgain_out, dimg_out,
    loss_buf, dtok_buf, dw_buf, dgain_buf, dimg_buf, ins, outs,
):
    trips = [
        (dtok.at[rows, :], dtok_buf.at[rows, :], dtok_out.at[rows, :])
        for rows in [pl.ds(i * 64, 64) for i in range(8)]
    ]
    trips += [
        (dw, dw_buf, dw_out), (dimg, dimg_buf, dimg_out), (dgain, dgain_buf, dgain_out), (loss, loss_buf, loss_out)
    ]
    reads, writes = [], []
    for i, (src, buf, _) in enumerate(trips):
        cp = pltpu.make_async_copy(src, buf, ins.at[i])
        cp.start()
        reads.append(cp)
    for i, (_, buf, dst) in enumerate(trips):
        reads[i].wait()
        cp = pltpu.make_async_copy(buf, dst, outs.at[i])
        cp.start()
        writes.append(cp)
    for cp in writes:
        cp.wait()


def per_device(tokens, segment_ids, owners, images, weight, gain, head, logit_params):
    vmem = pl.BlockSpec(memory_space=pltpu.VMEM)
    hbm = pl.BlockSpec(memory_space=pl.ANY)
    dma = pltpu.SemaphoreType.DMA
    shapes = (
        jax.ShapeDtypeStruct((1, 16), f32),
        jax.ShapeDtypeStruct((ROWS, DT), bf16),
        jax.ShapeDtypeStruct((16, DT), f32),
        jax.ShapeDtypeStruct((16, 128), f32),
        jax.ShapeDtypeStruct((16, E), f32),
    )
    held = pl.pallas_call(
        kernel,
        out_shape=shapes,
        in_specs=[hbm, hbm, hbm, hbm, hbm, hbm, hbm, pl.BlockSpec(memory_space=pltpu.SMEM)],
        out_specs=(vmem, hbm, hbm, vmem, hbm),
        scratch_shapes=[
            pltpu.VMEM((ROWS, DT), bf16),
            pltpu.VMEM((DT, DT), bf16),
            pltpu.VMEM((DT, E), bf16),
            pltpu.VMEM((4, 2, 2, 4, 2, 16, E), bf16),
            pltpu.VMEM((ROWS, 128), f32),
            pltpu.VMEM((ROWS, 128), f32),
            pltpu.VMEM((ROWS, 1), f32),
            pltpu.VMEM((CAPS, DT), f32),
            pltpu.VMEM((CAPS, DT), f32),
            pltpu.VMEM((2 * CAPS, DT), bf16),
            pltpu.VMEM((CAPS, DT), bf16),
            pltpu.VMEM((NC, 2, CAPS, 128), bf16),
            pltpu.VMEM((NC, 2, CAPS, 128), bf16),
            pltpu.VMEM((NC, CAPS, PW), bf16),
            pltpu.VMEM((CAPS, DT), bf16),
            pltpu.VMEM((4 * CAPS, DT), bf16),
            pltpu.VMEM((1, ROWS), jnp.int32),
            pltpu.VMEM((1, CAPS), jnp.int32),
            pltpu.VMEM((16, E), bf16),
            pltpu.VMEM((1, DT), f32),
            pltpu.VMEM((16, DT), f32),
            pltpu.VMEM((16, E), f32),
            pltpu.VMEM((ROWS, DT), bf16),
            pltpu.VMEM((GR, E), f32),
            pltpu.VMEM((SLOTS, 512), bf16),
            pltpu.VMEM((GR + CAPS, 512), bf16),
            pltpu.VMEM((GR + CAPS, E), f32),
            pltpu.VMEM((SLOTS, 1), f32),
            pltpu.VMEM((NR, 16, E), bf16),
            pltpu.VMEM((NR, 16, E), bf16),
            pltpu.VMEM((NR, 16, E), bf16),
            pltpu.VMEM((NR, 16, E), bf16),
            pltpu.VMEM((NR, 8, 128), f32),
            pltpu.VMEM((NC, 8, 128), f32),
            dma((5,)),
            dma((DT // TN,)),
            dma((4,)),
            dma((4,)),
            dma((DT // TN + 1,)),
            dma((PARTS, 2, 3)),
            dma((PARTS, 2, 3)),
            dma((PARTS, 4, 3)),
            dma((PARTS, 4, 3)),
            dma((PARTS, 4)),
            dma((PARTS, 4)),
            dma((3,)),
            dma((3,)),
            dma((4,)),
            dma((4,)),
            dma((NC - 1,)),
            dma((NC - 1,)),
            dma((NR - 1,)),
            dma((NR - 1,)),
            dma((NR - 1,)),
            dma((NR - 1,)),
            dma((NR - 1,)),
            dma((NR - 1,)),
            dma((NC - 1,)),
            dma((NC - 1,)),
        ],
        compiler_params=pltpu.CompilerParams(
            collective_id=0, has_side_effects=True, vmem_limit_bytes=56 * 1024 * 1024
        ),
    )(tokens, weight, head, segment_ids, owners, images, gain.reshape(1, DT), logit_params)
    loss, d_tokens, d_weight, d_gain, d_images = pl.pallas_call(
        hand_over,
        out_shape=shapes,
        in_specs=[hbm] * 5,
        out_specs=(hbm,) * 5,
        scratch_shapes=[pltpu.VMEM(out.shape, out.dtype) for out in shapes] + [dma((12,)), dma((12,))],
        compiler_params=pltpu.CompilerParams(vmem_limit_bytes=56 * 1024 * 1024),
    )(*held)
    return loss.reshape(16), d_tokens, d_weight, d_gain.reshape(DT), d_images


def solution(mesh):
    rows = P(("blk", "dp"), None)
    return jax.shard_map(
        per_device,
        mesh=mesh,
        in_specs=(rows, rows, rows, rows, P(), P(), P(), P()),
        out_specs=(P(("blk", "dp")), rows, rows, P(), rows),
        check_vma=False,
    )
```
